256 devices in a mesh: rep: 16 (over z, x_lo), col: 16 (over y, x_hi, core).
Axes of the slice: x: 4 (x_hi: 2, x_lo: 2; x = x_hi * 2 + x_lo), y: 4, z: 8, core: 2. Of those that a mesh axis runs over, the one named last changes fastest.
Arguments:
- activations: bfloat16 [16384, 4096], P('rep', 'col'), may hold values from -6 to 6
- out_grads: bfloat16 [16384, 8192], P('rep', 'col'), may hold values from -0.1875 to 0.1875
- carried_error: bfloat16 [16, 4096, 8192], P('rep', None, 'col'), may hold values from -6 to 6
- seed_value: int32 [1], replicated, may hold values from 0 to 999999
Outputs:
- p_factor: float32 [4096, 32], replicated
- q_factor: float32 [8192, 32], P('col')
- new_error: bfloat16 [16, 4096, 8192], P('rep', None, 'col')
The draws below stay inside these ranges and needn't reach their ends.
All inputs are finite; a program needn't handle non-finite values.
Results may differ from the reference program's by a relative error of at most 0.01.
Values may be sent and summed in bfloat16 or wider, within the bound.
A program may use at most 64 MiB of HBM per device.

```python
import jax
import jax.numpy as jnp
from jax import lax

DIN = 4096
DOUT = 8192
RANK = 32
TOK = 1024
TOKENS = 16384
N_REP = 16


def block_levels(stream_key, shape, shards, low, high):
    def one(position, parts):
        heights = jax.random.uniform(jax.random.fold_in(jax.random.fold_in(stream_key, 6), position), (parts,), jnp.float32, low / len(shards), high / len(shards))
        return jnp.repeat(jnp.exp(heights), shape[position] // parts).reshape((-1,) + (1,) * (len(shape) - position - 1))

    factor_of = one(*shards[0])
    for cut in shards[1:]:
        factor_of = factor_of * one(*cut)
    return factor_of


def normal_values(own_key, dims, spread, reach, pieces=(), kind=jnp.bfloat16):
    result = spread * jax.random.normal(own_key, dims, jnp.float32)
    if pieces:
        result = result * block_levels(own_key, dims, pieces, -0.22, 0.18)
    return jnp.clip(result, -reach, reach).astype(kind)


def setup_inputs(seed: int = 0) -> dict:
    arg_keys = jax.random.split(jax.random.key(seed), 5)
    return {
        "activations": normal_values(arg_keys[0], (TOKENS, DIN), 1.0, 6.0, ((0, 16), (1, 16))),
        "out_grads": normal_values(arg_keys[1], (TOKENS, DOUT), (TOK ** -0.5), 0.1875, ((0, 16), (1, 16))),
        "carried_error": normal_values(arg_keys[2], (N_REP, DIN, DOUT), 1.0, 6.0, ((0, 16), (2, 16))),
        "seed_value": jax.random.randint(arg_keys[3], (1,), 0, 1000000).astype(jnp.int32),
    }


def seeded_start(seed_scalar, offset, amount):
    row_ids = offset + lax.iota(jnp.int32, amount)
    hashed = row_ids[:, None] * RANK + lax.iota(jnp.int32, RANK)[None, :]
    hashed = hashed * 1103515245 + seed_scalar * 12345 + 7
    hashed = jnp.bitwise_xor(hashed, jnp.right_shift(hashed, 13))
    hashed = hashed * 747796405 + 1013904223
    hashed = jnp.bitwise_xor(hashed, jnp.right_shift(hashed, 16))
    return jnp.bitwise_and(hashed, 65535).astype(jnp.float32) / 32768.0 - 1.0

def reference(activations, out_grads, carried_error, seed_value):
    start_q = seeded_start(seed_value[0], 0, DOUT)
    inputs = activations.reshape(N_REP, TOK, DIN)
    outputs = out_grads.reshape(N_REP, TOK, DOUT)

    def form(index):
        product = lax.dot_general(inputs[index].astype(jnp.float32), outputs[index].astype(jnp.float32), (((0,), (0,)), ((), ())), preferred_element_type=jnp.float32)
        return product + carried_error[index].astype(jnp.float32)
    combined = lax.map(form, jnp.arange(N_REP))
    projected = jnp.einsum('rij,jk->ik', combined, start_q, precision=lax.Precision.HIGHEST)
    gram_matrix = jnp.dot(projected.T, projected, precision=lax.Precision.HIGHEST)
    factor_lower = jnp.linalg.cholesky(gram_matrix)
    basis = jax.scipy.linalg.solve_triangular(factor_lower, projected.T, lower=True).T
    q_factor = jnp.einsum('rij,ik->jk', combined, basis, precision=lax.Precision.HIGHEST) / N_REP
    rebuilt = jnp.dot(basis, q_factor.T, precision=lax.Precision.HIGHEST)
    new_error = (combined - rebuilt[None]).astype(jnp.bfloat16)
    return (basis * jnp.sqrt(jnp.float32(DIN)), q_factor, new_error)
```

```python
import functools

import jax
import jax.numpy as jnp
from jax import lax
from jax.experimental import pallas as pl
from jax.experimental.pallas import tpu as pltpu
from jax.sharding import PartitionSpec as P

RANK = 32
F32, BF16 = jnp.float32, jnp.bfloat16
MESH = pl.DeviceIdType.MESH
NN = (((1,), (0,)), ((), ()))
NT = (((1,), (1,)), ((), ()))
TN = (((0,), (0,)), ((), ()))
HIGH = lax.Precision.HIGHEST
CHUNKS = 4
TOK = 1024
ROWS = TOK // CHUNKS


def dot(a, b, dims, **kw):
    return lax.dot_general(a, b, dims, preferred_element_type=F32, **kw)


def split(x):
    hi = x.astype(BF16)
    return hi, (x - hi.astype(F32)).astype(BF16)


def fold(r):
    return r[:RANK] + r[RANK:]


def start_factor(seed, first):
    i = first + lax.broadcasted_iota(jnp.int32, (RANK, 512), 1)
    j = lax.broadcasted_iota(jnp.int32, (RANK, 512), 0)
    h = i * RANK + j
    h = h * 1103515245 + seed * 12345 + 7
    h = jnp.bitwise_xor(h, jnp.right_shift(h, 13))
    h = h * 747796405 + 1013904223
    h = jnp.bitwise_xor(h, jnp.right_shift(h, 16))
    return jnp.bitwise_and(h, 65535).astype(F32) / 32768.0 - 1.0


def lower_inverse(gram):
    lane = lax.broadcasted_iota(jnp.int32, (RANK, RANK), 1)
    row = lax.broadcasted_iota(jnp.int32, (RANK, RANK), 0)
    a = jnp.concatenate([gram, jnp.where(lane == row, 1.0, 0.0).astype(F32)], axis=1)
    rows = lax.broadcasted_iota(jnp.int32, (RANK, 2 * RANK), 0)
    for k in range(RANK):
        factor = jnp.where(rows > k, a[:, k : k + 1] / a[k : k + 1, k : k + 1], 0.0)
        a = a - factor * a[k : k + 1, :]
    pivots = jnp.sum(jnp.where(lane == row, a[:, :RANK], 0.0), axis=1, keepdims=True)
    return a[:, RANK:] / jnp.sqrt(pivots)


def kernel(
    seed_ref, a_hbm, g_hbm, e_hbm,
    pt_out, qt_out, err_out,
    e, g, agat, abuf, comb, qhl, part, sibbuf, rsbuf, upart, usib, ubuf, agu, zbuf, pall, pt, p64, b96, q96, wpart, wbuf, wall,
    load_s, gs, gr, ss, sr, swap_s, us, ur, rus, rur, aus, aur, uss, usr, es, er, rss, rsr, zs, zr, ps, pr, pss, psr, ws, wr, was, war,
):
    rep, col = lax.axis_index("rep"), lax.axis_index("col")
    z, xl = rep // 2, rep % 2
    y, xh, c = col // 4, (col // 2) % 2, col % 2
    x = xh * 2 + xl
    p = y * 4 + x
    other = 1 - c

    def dev(z_, x_, y_, c_):
        return (z_ * 2 + x_ % 2, (y_ * 2 + x_ // 2) * 2 + c_)

    sib = (rep, col - c + other)
    plane = [(dx, dy) for dy in (2, 1, 3, 0) for dx in (2, 1, 3, 0) if (dx, dy) != (0, 0)]
    colp = [(dx, dy) for dy in (2, 1, 3, 0) for dx in (2, 0) if (dx, dy) != (0, 0)]
    zline = [4, 3, 5, 2, 6, 1, 7]
    repp = [(dx, dz) for dz in (4, 3, 5, 2, 6, 1, 7, 0) for dx in (1, 0) if (dx, dz) != (0, 0)]

    def plane_dev(dx, dy):
        return dev(z, (x + dx) % 4, (y + dy) % 4, c)

    def z_dev(dz):
        return dev((z + dz) % 8, x, y, c)

    barrier = pltpu.get_barrier_semaphore()
    for peer in [sib] + [plane_dev(*d) for d in plane] + [z_dev(d) for d in zline]:
        pl.semaphore_signal(barrier, inc=1, device_id=peer, device_id_type=MESH)

    loads = [
        pltpu.make_async_copy(g_hbm, g, load_s.at[0]),
        pltpu.make_async_copy(a_hbm, agat.at[col], load_s.at[1]),
        pltpu.make_async_copy(e_hbm.at[0], e, load_s.at[2]),
        pltpu.make_async_copy(a_hbm.at[:, pl.ds(pl.multiple_of(xl * 128, 128), 128)], abuf.at[xl], load_s.at[3]),
    ]
    for copy in loads:
        copy.start()

    sent = []

    def send(src, dst, s, r, to):
        copy = pltpu.make_async_remote_copy(src_ref=src, dst_ref=dst, send_sem=s, recv_sem=r, device_id=to, device_id_type=MESH)
        copy.start()
        sent.append(copy)
        return copy

    q_hi, q_lo = split(start_factor(seed_ref[0], col * 512))
    qhl[pl.ds(0, RANK), :] = q_hi
    qhl[pl.ds(RANK, RANK), :] = q_lo
    loads[0].wait()
    u = fold(dot(qhl[...], g[...], NT))
    for i in range(4):
        for j in range(4):
            upart[j % 2, i * 2 + j // 2] = u[8 * i : 8 * i + 8, 256 * j : 256 * j + 256]
    loads[2].wait()
    for b in range(16):
        r = fold(dot(qhl[...], e[pl.ds(b * 256, 256), :], NT))
        part[b % 2, (b // 2) * 2] = r[:, :128]
        part[b % 2, (b // 2) * 2 + 1] = r[:, 128:]
    loads[1].wait()
    loads[3].wait()
    pl.semaphore_wait(barrier, 1 + len(plane) + len(zline))

    u_sib = send(upart.at[other], usib, us.at[0], ur.at[0], sib)
    e_sib = send(part.at[other], sibbuf, es.at[0], er.at[0], sib)
    swap = send(
        a_hbm.at[:, pl.ds(pl.multiple_of((1 - xl) * 128, 128), 128)], abuf.at[xl], swap_s.at[0], swap_s.at[1],
        dev(z, xh * 2 + 1 - xl, y, c),
    )

    yp, ym = (y + 1) % 4, (y + 3) % 4
    up, down, mirror = dev(z, x, yp, c), dev(z, x, ym, c), dev(z, (x + 2) % 4, y, c)

    def block(y_, xh_):
        return (y_ * 2 + xh_) * 2 + c

    own, b_up, b_down, b_far = col, block(yp, xh), block(ym, xh), block((y + 2) % 4, xh)
    m_own, m_up, m_down, m_far = block(y, 1 - xh), block(yp, 1 - xh), block(ym, 1 - xh), block((y + 2) % 4, 1 - xh)

    def piece(b, j):
        return agat.at[b, pl.ds(j * ROWS, ROWS)]

    moves = {}

    def relay(flow, b, j, to):
        moves[flow, j] = send(piece(b, j), piece(b, j), gs.at[flow, j], gr.at[flow, j], to)

    def to_sib(slot, b, j):
        moves[8 + slot, j] = send(piece(b, j), piece(b, j), ss.at[slot, j], sr.at[slot, j], sib)

    def arrive(flow, j):
        moves[flow, j].wait_recv()

    def first(j):
        relay(0, own, j, up)
        relay(1, own, j, down)
        relay(2, own, j, mirror)
        to_sib(0, own, j)

    def second(j):
        arrive(2, j)
        relay(5, m_own, j, up)
        relay(6, m_own, j, down)
        arrive(1, j)
        arrive(0, j)
        if j < CHUNKS // 2:
            relay(3, b_up, j, down)
        else:
            relay(4, b_down, j, up)
        to_sib(1, b_up, j)
        to_sib(2, b_down, j)
        to_sib(3, m_own, j)

    def third(j):
        arrive(3 if j < CHUNKS // 2 else 4, j)
        relay(7, b_far, j, mirror)
        to_sib(4, b_far, j)

    def fourth(j):
        arrive(5, j)
        to_sib(5, m_down, j)
        arrive(6, j)
        to_sib(6, m_up, j)

    def fifth(j):
        arrive(7, j)
        to_sib(7, m_far, j)

    def product(b):
        at = pl.ds(pl.multiple_of(b * 256, 256), 256)
        comb[at, :] = dot(agat[b], g[...], TN) + e[at, :].astype(F32)

    def both(slot, b):
        product(b)
        for j in range(CHUNKS):
            arrive(8 + slot, j)
        product(b - c + other)

    first(0)
    u_sib.wait_recv()
    mine = upart[c] + usib[...]
    ubuf[pl.ds(0, 8)] = mine
    k = y * 2 + xh
    ru = [
        send(ubuf.at[((y + dy) % 4) * 2 + ((x + dx) % 4) // 2], ubuf.at[8 + k], rus.at[n], rur.at[n], plane_dev(dx, dy))
        for n, (dx, dy) in enumerate(colp)
    ]
    first(1)
    e_sib.wait_recv()
    part[c] = part[c] + sibbuf[...]
    re = [
        send(part.at[c, ((y + dy) % 4) * 4 + (x + dx) % 4], rsbuf.at[p], rss.at[n], rsr.at[n], plane_dev(dx, dy))
        for n, (dx, dy) in enumerate(plane)
    ]
    rsbuf[p] = part[c, p]
    first(2)
    first(3)
    ubuf[8 + k] = ubuf[k]
    for copy in ru:
        copy.wait_recv()
    total = ubuf[8]
    for n in range(1, 8):
        total = total + ubuf[8 + n]
    agu[c, p] = total
    au = [send(agu.at[c, p], agu.at[c, p], aus.at[n], aur.at[n], plane_dev(dx, dy)) for n, (dx, dy) in enumerate(plane)]
    second(0)
    for copy in re:
        copy.wait_recv()
    e_slice = rsbuf[0]
    for n in range(1, 16):
        e_slice = e_slice + rsbuf[n]
    second(1)
    swap.wait_recv()
    for copy in au:
        copy.wait_recv()
    u_fwd = send(agu.at[c], agu.at[c], uss.at[0], usr.at[0], sib)
    u_fwd.wait_recv()
    acc = e_slice
    for r in range(2):
        ut = jnp.concatenate(
            [jnp.concatenate([agu[j % 2, i * 4 + (j // 2) * 2 + r] for j in range(4)], axis=1) for i in range(4)], axis=0
        )
        acc = acc + fold(dot(jnp.concatenate(split(ut), axis=0), abuf[r], NN))
    zbuf[z] = acc
    zc = [send(zbuf.at[z], zbuf.at[z], zs.at[n], zr.at[n], z_dev(d)) for n, d in enumerate(zline)]
    second(2)
    second(3)
    both(0, own)
    third(0)
    third(1)
    for copy in zc:
        copy.wait_recv()
    total = zbuf[0]
    for n in range(1, 8):
        total = total + zbuf[n]
    pall[c, p] = total
    pc = [send(pall.at[c, p], pall.at[c, p], ps.at[n], pr.at[n], plane_dev(dx, dy)) for n, (dx, dy) in enumerate(plane)]
    both(1, b_up)
    both(2, b_down)
    both(3, m_own)
    third(2)
    third(3)
    for copy in pc:
        copy.wait_recv()
    p_fwd = send(pall.at[c], pall.at[c], pss.at[0], psr.at[0], sib)
    fourth(0)
    fourth(1)
    fifth(0)
    fifth(1)
    p_fwd.wait_recv()
    for cc in range(2):
        for pp in range(16):
            s = 4 * (pp // 2) + 2 * cc + pp % 2
            v = pall[cc, pp]
            hi, lo = split(v)
            pt[:, pl.ds(s * 128, 128)] = v
            p64[pl.ds(0, RANK), pl.ds(s * 128, 128)] = hi
            p64[pl.ds(RANK, RANK), pl.ds(s * 128, 128)] = lo
    both(4, b_far)
    for j in range(2, CHUNKS):
        fourth(j)
        fifth(j)
    both(5, m_down)
    both(6, m_up)
    both(7, m_far)

    w = jnp.zeros((2 * RANK, 512), F32)
    for b in range(8):
        w = w + dot(p64[:, pl.ds(b * 512, 512)], comb[pl.ds(b * 512, 512), :].astype(BF16), NN)
    w = fold(w)
    for i in range(4):
        for j in range(4):
            wpart[i * 4 + j] = w[8 * i : 8 * i + 8, 128 * j : 128 * j + 128]

    def rep_dev(dx, dz):
        return dev((z + dz) % 8, xh * 2 + (xl + dx) % 2, y, c)

    wc = [
        send(wpart.at[((z + dz) % 8) * 2 + (xl + dx) % 2], wbuf.at[rep], ws.at[n], wr.at[n], rep_dev(dx, dz))
        for n, (dx, dz) in enumerate(repp)
    ]
    wbuf[rep] = wpart[rep]
    inverse = lower_inverse(dot(pt[...], pt[...], NT, precision=HIGH))
    for copy in wc:
        copy.wait_recv()
    total = wbuf[0]
    for n in range(1, 16):
        total = total + wbuf[n]
    wall[rep] = total
    wa = [send(wall.at[rep], wall.at[rep], was.at[n], war.at[n], rep_dev(dx, dz)) for n, (dx, dz) in enumerate(repp)]
    basis = dot(inverse, pt[...], NN, precision=HIGH)
    pt_out[...] = basis * 64.0
    b_hi, b_lo = split(basis)
    b96[pl.ds(0, RANK), :] = b_hi
    b96[pl.ds(RANK, RANK), :] = b_lo
    b96[pl.ds(2 * RANK, RANK), :] = b_hi
    for copy in wa:
        copy.wait_recv()
    w = jnp.concatenate([jnp.concatenate([wall[i * 4 + j] for j in range(4)], axis=1) for i in range(4)], axis=0)
    qt = dot(inverse, w, NN, precision=HIGH) * (1.0 / 16.0)
    qt_out[...] = qt
    f_hi, f_lo = split(qt)
    q96[pl.ds(0, RANK), :] = f_hi
    q96[pl.ds(RANK, RANK), :] = f_hi
    q96[pl.ds(2 * RANK, RANK), :] = f_lo
    for b in range(16):
        at = pl.ds(b * 256, 256)
        err_out[0, at, :] = (comb[at, :] - dot(b96[:, at], q96[...], TN)).astype(BF16)
    for copy in sent:
        copy.wait_send()


def local(activations, out_grads, carried_error, seed_value):
    vmem, any_ = pl.BlockSpec(memory_space=pltpu.VMEM), pl.BlockSpec(memory_space=pl.ANY)
    dma, shape = pltpu.SemaphoreType.DMA, jax.ShapeDtypeStruct
    V = pltpu.VMEM
    pt, qt, err = pl.pallas_call(
        kernel,
        name="round",
        out_shape=(shape((RANK, 4096), F32), shape((RANK, 512), F32), shape((1, 4096, 512), BF16)),
        in_specs=[pl.BlockSpec(memory_space=pltpu.SMEM), any_, any_, any_],
        out_specs=(vmem, vmem, vmem),
        scratch_shapes=[
            V((4096, 512), BF16), V((TOK, 512), BF16), V((16, TOK, 256), BF16), V((2, TOK, 128), BF16), V((4096, 512), F32),
            V((2 * RANK, 512), BF16), V((2, 16, RANK, 128), F32), V((16, RANK, 128), F32), V((16, RANK, 128), F32),
            V((2, 8, 8, 256), F32), V((8, 8, 256), F32), V((16, 8, 256), F32), V((2, 16, 8, 256), F32),
            V((8, RANK, 128), F32), V((2, 16, RANK, 128), F32), V((RANK, 4096), F32), V((2 * RANK, 4096), BF16),
            V((3 * RANK, 4096), BF16), V((3 * RANK, 512), BF16), V((16, 8, 128), F32), V((16, 8, 128), F32), V((16, 8, 128), F32),
            dma((4,)), dma((8, CHUNKS)), dma((8, CHUNKS)), dma((8, CHUNKS)), dma((8, CHUNKS)), dma((2,)),
            dma((1,)), dma((1,)), dma((7,)), dma((7,)), dma((15,)), dma((15,)), dma((1,)), dma((1,)), dma((1,)), dma((1,)),
            dma((15,)), dma((15,)), dma((7,)), dma((7,)), dma((15,)), dma((15,)), dma((1,)), dma((1,)),
            dma((15,)), dma((15,)), dma((15,)), dma((15,)),
        ],
        compiler_params=pltpu.CompilerParams(collective_id=1, has_side_effects=True, vmem_limit_bytes=56 << 20),
        cost_estimate=pl.CostEstimate(flops=4_600_000_000, bytes_accessed=10_000_000, transcendentals=0),
    )(seed_value, activations, out_grads, carried_error)
    return pt.T, qt.T, err


def solution(mesh):
    return jax.shard_map(
        local,
        mesh=mesh,
        in_specs=(P("rep", "col"), P("rep", "col"), P("rep", None, "col"), P()),
        out_specs=(P(), P("col", None), P("rep", None, "col")),
        check_vma=False,
    )
```

```python
import functools

import jax
import jax.numpy as jnp
from jax import lax
from jax.experimental import pallas as pl
from jax.experimental.pallas import tpu as pltpu
from jax.sharding import PartitionSpec as P

RANK = 32
F32, BF16 = jnp.float32, jnp.bfloat16
MESH = pl.DeviceIdType.MESH
NN = (((1,), (0,)), ((), ()))
NT = (((1,), (1,)), ((), ()))
TN = (((0,), (0,)), ((), ()))
HIGH = lax.Precision.HIGHEST
CHUNKS = 4
TOK = 1024
ROWS = TOK // CHUNKS
PIECES = 8


def dot(a, b, dims, **kw):
    return lax.dot_general(a, b, dims, preferred_element_type=F32, **kw)


def split(x):
    hi = x.astype(BF16)
    return hi, (x - hi.astype(F32)).astype(BF16)


def fold(r):
    return r[:RANK] + r[RANK:]


def start_factor(seed, first):
    i = first + lax.broadcasted_iota(jnp.int32, (RANK, 512), 1)
    j = lax.broadcasted_iota(jnp.int32, (RANK, 512), 0)
    h = i * RANK + j
    h = h * 1103515245 + seed * 12345 + 7
    h = jnp.bitwise_xor(h, jnp.right_shift(h, 13))
    h = h * 747796405 + 1013904223
    h = jnp.bitwise_xor(h, jnp.right_shift(h, 16))
    return jnp.bitwise_and(h, 65535).astype(F32) / 32768.0 - 1.0


def lower_inverse(gram):
    lane = lax.broadcasted_iota(jnp.int32, (RANK, RANK), 1)
    row = lax.broadcasted_iota(jnp.int32, (RANK, RANK), 0)
    a = jnp.concatenate([gram, jnp.where(lane == row, 1.0, 0.0).astype(F32)], axis=1)
    rows = lax.broadcasted_iota(jnp.int32, (RANK, 2 * RANK), 0)
    for k in range(RANK):
        factor = jnp.where(rows > k, a[:, k : k + 1] / a[k : k + 1, k : k + 1], 0.0)
        a = a - factor * a[k : k + 1, :]
    pivots = jnp.sum(jnp.where(lane == row, a[:, :RANK], 0.0), axis=1, keepdims=True)
    return a[:, RANK:] / jnp.sqrt(pivots)


def kernel(
    seed_ref, a_hbm, g_hbm, e_hbm,
    comb, b96, q96, pt_out, qt_out,
    e, g, agat, abuf, qhl, part, sibbuf, rsbuf, upart, usib, ubuf, agu, zbuf, pall, pt, p64, wpart, wbuf, wall, vown, vmir,
    load_s, gs, gr, ss, sr, swap_s, us, ur, rus, rur, aus, aur, uss, usr, es, er, rss, rsr, zs, zr, ps, pr, pss, psr, ws, wr, was, war, vs, vr,
):
    rep, col = lax.axis_index("rep"), lax.axis_index("col")
    z, xl = rep // 2, rep % 2
    y, xh, c = col // 4, (col // 2) % 2, col % 2
    x = xh * 2 + xl
    p = y * 4 + x
    other = 1 - c

    def dev(z_, x_, y_, c_):
        return (z_ * 2 + x_ % 2, (y_ * 2 + x_ // 2) * 2 + c_)

    sib = (rep, col - c + other)
    plane = [(dx, dy) for dy in (2, 1, 3, 0) for dx in (2, 1, 3, 0) if (dx, dy) != (0, 0)]
    colp = [(dx, dy) for dy in (2, 1, 3, 0) for dx in (2, 0) if (dx, dy) != (0, 0)]
    zline = [4, 3, 5, 2, 6, 1, 7]
    repp = [(dx, dz) for dz in (4, 3, 5, 2, 6, 1, 7, 0) for dx in (1, 0) if (dx, dz) != (0, 0)]

    def plane_dev(dx, dy):
        return dev(z, (x + dx) % 4, (y + dy) % 4, c)

    def z_dev(dz):
        return dev((z + dz) % 8, x, y, c)

    barrier = pltpu.get_barrier_semaphore()
    for peer in [sib] + [plane_dev(*d) for d in plane] + [z_dev(d) for d in zline]:
        pl.semaphore_signal(barrier, inc=1, device_id=peer, device_id_type=MESH)

    loads = [
        pltpu.make_async_copy(g_hbm, g, load_s.at[0]),
        pltpu.make_async_copy(a_hbm, agat.at[col], load_s.at[1]),
        pltpu.make_async_copy(e_hbm.at[0], e, load_s.at[2]),
        pltpu.make_async_copy(a_hbm.at[:, pl.ds(pl.multiple_of(xl * 128, 128), 128)], abuf.at[xl], load_s.at[3]),
    ]
    for copy in loads:
        copy.start()

    sent = []

    def send(src, dst, s, r, to, keep=True):
        copy = pltpu.make_async_remote_copy(src_ref=src, dst_ref=dst, send_sem=s, recv_sem=r, device_id=to, device_id_type=MESH)
        copy.start()
        if keep:
            sent.append(copy)
        return copy

    loads[0].wait()
    q_hi, q_lo = split(start_factor(seed_ref[0], col * 512))
    qhl[pl.ds(0, RANK), :] = q_hi
    qhl[pl.ds(RANK, RANK), :] = q_lo
    u = fold(dot(qhl[...], g[...], NT))
    for i in range(4):
        for j in range(4):
            upart[j % 2, i * 2 + j // 2] = u[8 * i : 8 * i + 8, 256 * j : 256 * j + 256]
    loads[1].wait()
    loads[3].wait()
    pl.semaphore_wait(barrier, 1 + len(plane) + len(zline))

    yp, ym = (y + 1) % 4, (y + 3) % 4
    up, down, mirror = dev(z, x, yp, c), dev(z, x, ym, c), dev(z, (x + 2) % 4, y, c)

    def block(y_, xh_):
        return (y_ * 2 + xh_) * 2 + c

    own, b_up, b_down, b_far = col, block(yp, xh), block(ym, xh), block((y + 2) % 4, xh)
    m_own, m_up, m_down, m_far = block(y, 1 - xh), block(yp, 1 - xh), block(ym, 1 - xh), block((y + 2) % 4, 1 - xh)
    blocks = dict(own=own, up=b_up, down=b_down, far=b_far, m_own=m_own, m_up=m_up, m_down=m_down, m_far=m_far)
    slots = list(blocks)
    lanes = (up, down, mirror)
    there = (
        dict(own="down", down="far", m_own="m_down"),
        dict(own="up", up="far", m_own="m_up"),
        dict(own="m_own", far="m_far"),
    )
    moves, passed = {}, {}

    def piece(b, j):
        return agat.at[b, pl.ds(j * ROWS, ROWS)]

    def to_sib(name, j):
        at, n = piece(blocks[name], j), slots.index(name)
        passed[name, j] = send(at, at, ss.at[n, j], sr.at[n, j], sib)

    def go(lane, name, j):
        at, n = piece(blocks[name], j), sum(1 for m in moves if m[0] == lane)
        moves[lane, there[lane][name], j] = send(at, at, gs.at[lane, n], gr.at[lane, n], lanes[lane])

    def got(lane, name, j):
        moves[lane, name, j].wait_recv()
        to_sib(name, j)

    def swap(n):
        rows = pl.ds(n * ROWS, ROWS)
        return send(
            a_hbm.at[rows, pl.ds(pl.multiple_of((1 - xl) * 128, 128), 128)], abuf.at[xl, rows], swap_s.at[n], swap_s.at[CHUNKS + n],
            dev(z, xh * 2 + 1 - xl, y, c),
        )

    u_sib = send(upart.at[other], usib, us.at[0], ur.at[0], sib)
    for j in range(CHUNKS):
        to_sib("own", j)

    def product(b):
        at = pl.ds(pl.multiple_of(b * 256, 256), 256)
        comb[at, :] = dot(agat[b], g[...], TN) + e[at, :].astype(F32)

    def both(name):
        b = blocks[name]
        product(b)
        for j in range(CHUNKS):
            passed[name, j].wait_recv()
        product(b - c + other)

    u_sib.wait_recv()
    ubuf[pl.ds(0, 8)] = upart[c] + usib[...]
    k = y * 2 + xh
    ru = [
        send(ubuf.at[((y + dy) % 4) * 2 + ((x + dx) % 4) // 2], ubuf.at[8 + k], rus.at[n], rur.at[n], plane_dev(dx, dy))
        for n, (dx, dy) in enumerate(colp)
    ]
    ubuf[8 + k] = ubuf[k]
    go(0, "own", 2)
    go(1, "own", 0)
    swaps = [swap(0), swap(1)]
    loads[2].wait()
    for b in range(16):
        r = fold(dot(qhl[...], e[pl.ds(b * 256, 256), :], NT))
        part[b % 2, (b // 2) * 2] = r[:, :128]
        part[b % 2, (b // 2) * 2 + 1] = r[:, 128:]
    e_sib = send(part.at[other], sibbuf, es.at[0], er.at[0], sib)
    for copy in ru:
        copy.wait_recv()
    total = ubuf[8]
    for n in range(1, 8):
        total = total + ubuf[8 + n]
    agu[c, p] = total
    au = [send(agu.at[c, p], agu.at[c, p], aus.at[n], aur.at[n], plane_dev(dx, dy)) for n, (dx, dy) in enumerate(plane)]
    e_sib.wait_recv()
    part[c] = part[c] + sibbuf[...]
    re = [
        send(part.at[c, ((y + dy) % 4) * 4 + (x + dx) % 4], rsbuf.at[p], rss.at[n], rsr.at[n], plane_dev(dx, dy))
        for n, (dx, dy) in enumerate(plane)
    ]
    rsbuf[p] = part[c, p]
    swaps += [swap(2), swap(3)]
    for n, j in enumerate((3, 0, 1)):
        go(0, "own", j)
        go(1, "own", (1, 2, 3)[n])
        go(2, "own", n)
    got(0, "down", 2)
    got(1, "up", 0)
    go(0, "down", 2)
    go(1, "up", 0)
    for copy in au:
        copy.wait_recv()
    u_fwd = send(agu.at[c], agu.at[c], uss.at[0], usr.at[0], sib)
    for copy in re:
        copy.wait_recv()
    acc = rsbuf[0]
    for n in range(1, 16):
        acc = acc + rsbuf[n]
    for copy in swaps:
        copy.wait_recv()
    u_fwd.wait_recv()
    for r in range(2):
        ut = jnp.concatenate(
            [jnp.concatenate([agu[j % 2, i * 4 + (j // 2) * 2 + r] for j in range(4)], axis=1) for i in range(4)], axis=0
        )
        acc = acc + fold(dot(jnp.concatenate(split(ut), axis=0), abuf[r], NN))
    zbuf[z] = acc
    zc = [send(zbuf.at[z], zbuf.at[z], zs.at[n], zr.at[n], z_dev(d)) for n, d in enumerate(zline)]
    both("own")
    got(0, "down", 3)
    got(1, "up", 1)
    got(2, "m_own", 0)
    for copy in zc:
        copy.wait_recv()
    total = zbuf[0]
    for n in range(1, 8):
        total = total + zbuf[n]
    pall[c, p] = total
    pc = [send(pall.at[c, p], pall.at[c, p], ps.at[n], pr.at[n], plane_dev(dx, dy)) for n, (dx, dy) in enumerate(plane)]
    go(0, "down", 3)
    go(1, "up", 1)
    go(2, "own", 3)
    for n, j in enumerate((0, 1)):
        got(0, "down", j)
        got(1, "up", j + 2)
        got(2, "m_own", j + 1)
    for j in range(3):
        go(0, "m_own", j)
        go(1, "m_own", j)
    got(0, "far", 2)
    got(1, "far", 0)
    go(2, "far", 2)
    for copy in pc:
        copy.wait_recv()
    p_fwd = send(pall.at[c], pall.at[c], pss.at[0], psr.at[0], sib)
    both("up")
    both("down")
    p_fwd.wait_recv()
    for cc in range(2):
        for pp in range(16):
            s = 4 * (pp // 2) + 2 * cc + pp % 2
            v = pall[cc, pp]
            hi, lo = split(v)
            pt[:, pl.ds(s * 128, 128)] = v
            p64[pl.ds(0, RANK), pl.ds(s * 128, 128)] = hi
            p64[pl.ds(RANK, RANK), pl.ds(s * 128, 128)] = lo
    got(0, "far", 3)
    got(1, "far", 1)
    both("far")

    v = jnp.zeros((2 * RANK, TOK), F32)
    for name in ("own", "up", "down", "far"):
        for b in (blocks[name], blocks[name] - c + other):
            v = v + dot(p64[:, pl.ds(pl.multiple_of(b * 256, 256), 256)], agat[b], NT)
    v = fold(v)
    for h in range(2):
        vown[h] = v[:, h * 512 : h * 512 + 512]
    v_far = send(vown.at[c], vmir.at[c], vs.at[0], vr.at[0], mirror)
    got(2, "m_own", 3)
    go(0, "m_own", 3)
    go(1, "m_own", 3)
    go(2, "far", 0)
    go(2, "far", 3)
    go(2, "far", 1)
    w = fold(dot(p64[...], e[...], NN))
    inverse = lower_inverse(dot(pt[...], pt[...], NT, precision=HIGH))
    v_far.wait_recv()
    v_fwd = send(vmir.at[c], vmir.at[c], vs.at[1], vr.at[1], sib)
    both("m_own")
    v_fwd.wait_recv()
    for h in range(2):
        w = w + fold(dot(jnp.concatenate(split(vown[h] + vmir[h]), axis=0), g[pl.ds(h * 512, 512), :], NN))
    for i in range(4):
        for j in range(4):
            wpart[i * 4 + j] = w[8 * i : 8 * i + 8, 128 * j : 128 * j + 128]

    def rep_dev(dx, dz):
        return dev((z + dz) % 8, xh * 2 + (xl + dx) % 2, y, c)

    wc = [
        send(wpart.at[((z + dz) % 8) * 2 + (xl + dx) % 2], wbuf.at[rep], ws.at[n], wr.at[n], rep_dev(dx, dz))
        for n, (dx, dz) in enumerate(repp)
    ]
    wbuf[rep] = wpart[rep]
    basis = dot(inverse, pt[...], NN, precision=HIGH)
    for j in range(3):
        got(0, "m_down", j)
        got(1, "m_up", j)
    got(2, "m_far", 2)
    got(2, "m_far", 0)
    for copy in wc:
        copy.wait_recv()
    total = wbuf[0]
    for n in range(1, 16):
        total = total + wbuf[n]
    wall[rep] = total
    wa = [send(wall.at[rep], wall.at[rep], was.at[n], war.at[n], rep_dev(dx, dz)) for n, (dx, dz) in enumerate(repp)]
    pt_out[...] = basis * 64.0
    b_hi, b_lo = split(basis)
    b96[pl.ds(0, RANK), :] = b_hi
    b96[pl.ds(RANK, RANK), :] = b_lo
    b96[pl.ds(2 * RANK, RANK), :] = b_hi
    got(0, "m_down", 3)
    got(1, "m_up", 3)
    got(2, "m_far", 3)
    got(2, "m_far", 1)
    both("m_up")
    both("m_down")
    both("m_far")
    for copy in wa:
        copy.wait_recv()
    w = jnp.concatenate([jnp.concatenate([wall[i * 4 + j] for j in range(4)], axis=1) for i in range(4)], axis=0)
    qt = dot(inverse, w, NN, precision=HIGH) * (1.0 / 16.0)
    qt_out[...] = qt
    f_hi, f_lo = split(qt)
    q96[pl.ds(0, RANK), :] = f_hi
    q96[pl.ds(RANK, RANK), :] = f_hi
    q96[pl.ds(2 * RANK, RANK), :] = f_lo
    for copy in sent:
        copy.wait_send()


def finish(comb, b96, q96, basis, factor, err_hbm, basis_hbm, factor_hbm, rounded, sems):
    copies = [pltpu.make_async_copy(basis, basis_hbm, sems.at[0]), pltpu.make_async_copy(factor, factor_hbm, sems.at[1])]
    for copy in copies:
        copy.start()
    step = 4096 // PIECES
    for b in range(PIECES):
        at = pl.ds(b * step, step)
        rounded[at, :] = (comb[at, :] - dot(b96[:, at], q96[...], TN)).astype(BF16)
        copies.append(pltpu.make_async_copy(rounded.at[at], err_hbm.at[0, at], sems.at[2 + b]))
        copies[-1].start()
    for copy in copies:
        copy.wait()


def local(activations, out_grads, carried_error, seed_value):
    vmem, any_ = pl.BlockSpec(memory_space=pltpu.VMEM), pl.BlockSpec(memory_space=pl.ANY)
    dma, shape = pltpu.SemaphoreType.DMA, jax.ShapeDtypeStruct
    V = pltpu.VMEM
    held = pl.pallas_call(
        kernel,
        name="round",
        out_shape=(V((4096, 512), F32), V((3 * RANK, 4096), BF16), V((3 * RANK, 512), BF16), V((RANK, 4096), F32), V((RANK, 512), F32)),
        in_specs=[pl.BlockSpec(memory_space=pltpu.SMEM), any_, any_, any_],
        out_specs=(vmem,) * 5,
        scratch_shapes=[
            V((4096, 512), BF16), V((TOK, 512), BF16), V((16, TOK, 256), BF16), V((2, TOK, 128), BF16),
            V((2 * RANK, 512), BF16), V((2, 16, RANK, 128), F32), V((16, RANK, 128), F32), V((16, RANK, 128), F32),
            V((2, 8, 8, 256), F32), V((8, 8, 256), F32), V((16, 8, 256), F32), V((2, 16, 8, 256), F32),
            V((8, RANK, 128), F32), V((2, 16, RANK, 128), F32), V((RANK, 4096), F32), V((2 * RANK, 4096), BF16),
            V((16, 8, 128), F32), V((16, 8, 128), F32), V((16, 8, 128), F32),
            V((2, RANK, 512), F32), V((2, RANK, 512), F32),
            dma((4,)), dma((3, 10)), dma((3, 10)), dma((8, CHUNKS)), dma((8, CHUNKS)), dma((2 * CHUNKS,)),
            dma((1,)), dma((1,)), dma((7,)), dma((7,)), dma((15,)), dma((15,)), dma((1,)), dma((1,)), dma((1,)), dma((1,)),
            dma((15,)), dma((15,)), dma((7,)), dma((7,)), dma((15,)), dma((15,)), dma((1,)), dma((1,)),
            dma((15,)), dma((15,)), dma((15,)), dma((15,)), dma((2,)), dma((2,)),
        ],
        compiler_params=pltpu.CompilerParams(collective_id=1, has_side_effects=True, vmem_limit_bytes=28 << 20),
        cost_estimate=pl.CostEstimate(flops=4_600_000_000, bytes_accessed=10_000_000, transcendentals=0),
    )(seed_value, *[pltpu.with_memory_space_constraint(a, pltpu.HBM) for a in (activations, out_grads, carried_error)])
    err, pt, qt = pl.pallas_call(
        finish,
        name="finish",
        out_shape=(shape((1, 4096, 512), BF16), shape((RANK, 4096), F32), shape((RANK, 512), F32)),
        in_specs=[vmem] * 5,
        out_specs=(any_,) * 3,
        scratch_shapes=[V((4096, 512), BF16), dma((2 + PIECES,))],
        compiler_params=pltpu.CompilerParams(vmem_limit_bytes=12 << 20),
    )(*[pltpu.with_memory_space_constraint(a, pltpu.VMEM) for a in held])
    return pt.T, qt.T, err


def solution(mesh):
    return jax.shard_map(
        local,
        mesh=mesh,
        in_specs=(P("rep", "col"), P("rep", "col"), P("rep", None, "col"), P()),
        out_specs=(P(), P("col", None), P("rep", None, "col")),
        check_vma=False,
    )
```

```python
import functools

import jax
import jax.numpy as jnp
from jax import lax
from jax.experimental import pallas as pl
from jax.experimental.pallas import tpu as pltpu
from jax.sharding import PartitionSpec as P

RANK = 32
F32, BF16 = jnp.float32, jnp.bfloat16
MESH = pl.DeviceIdType.MESH
NN = (((1,), (0,)), ((), ()))
NT = (((1,), (1,)), ((), ()))
TN = (((0,), (0,)), ((), ()))
HIGH = lax.Precision.HIGHEST
CHUNKS = 4
TOK = 1024
ROWS = TOK // CHUNKS
PIECES = 8


def dot(a, b, dims, **kw):
    return lax.dot_general(a, b, dims, preferred_element_type=F32, **kw)


def split(x):
    hi = x.astype(BF16)
    return hi, (x - hi.astype(F32)).astype(BF16)


def fold(r):
    return r[:RANK] + r[RANK:]


def start_factor(seed, first):
    i = first + lax.broadcasted_iota(jnp.int32, (RANK, 512), 1)
    j = lax.broadcasted_iota(jnp.int32, (RANK, 512), 0)
    h = i * RANK + j
    h = h * 1103515245 + seed * 12345 + 7
    h = jnp.bitwise_xor(h, jnp.right_shift(h, 13))
    h = h * 747796405 + 1013904223
    h = jnp.bitwise_xor(h, jnp.right_shift(h, 16))
    return jnp.bitwise_and(h, 65535).astype(F32) / 32768.0 - 1.0


def lower_inverse(gram):
    lane = lax.broadcasted_iota(jnp.int32, (RANK, RANK), 1)
    row = lax.broadcasted_iota(jnp.int32, (RANK, RANK), 0)
    a = jnp.concatenate([gram, jnp.where(lane == row, 1.0, 0.0).astype(F32)], axis=1)
    rows = lax.broadcasted_iota(jnp.int32, (RANK, 2 * RANK), 0)
    for k in range(RANK):
        factor = jnp.where(rows > k, a[:, k : k + 1] / a[k : k + 1, k : k + 1], 0.0)
        a = a - factor * a[k : k + 1, :]
    pivots = jnp.sum(jnp.where(lane == row, a[:, :RANK], 0.0), axis=1, keepdims=True)
    return a[:, RANK:] / jnp.sqrt(pivots)


def kernel(
    seed_ref, a_hbm, g_hbm, e_hbm,
    comb, b96, q96, pt_out, qt_out,
    e, g, agat, abuf, qhl, part, sibbuf, rsbuf, upart, usib, ubuf, agu, zbuf, pall, pt, p64, wpart, wbuf, wall, vown, vmir,
    load_s, gs, gr, ss, sr, swap_s, us, ur, rus, rur, aus, aur, uss, usr, es, er, rss, rsr, zs, zr, ps, pr, pss, psr, ws, wr, was, war, vs, vr,
):
    rep, col = lax.axis_index("rep"), lax.axis_index("col")
    z, xl = rep // 2, rep % 2
    y, xh, c = col // 4, (col // 2) % 2, col % 2
    x = xh * 2 + xl
    p = y * 4 + x
    other = 1 - c

    def dev(z_, x_, y_, c_):
        return (z_ * 2 + x_ % 2, (y_ * 2 + x_ // 2) * 2 + c_)

    sib = (rep, col - c + other)
    near = [(0, 1, 2), (0, 0, 2), (0, 1, 1), (0, 1, 3), (0, 0, 1), (0, 0, 3), (0, 1, 0)]
    far = [(1, fl, dy) for dy in (2, 1, 3, 0) for fl in (0, 1)]
    plane = far + near
    colp = [d for d in plane if d[1] == 0]
    zline = [4, 3, 5, 2, 6, 1, 7]
    repp = [(dx, dz) for dz in (4, 3, 5, 2, 6, 1, 7, 0) for dx in (1, 0) if (dx, dz) != (0, 0)]

    def plane_at(fh, fl, dy):
        return (y + dy) % 4, (xh + fh) % 2, (xl + fl) % 2

    def plane_dev(*d):
        y_, xh_, xl_ = plane_at(*d)
        return dev(z, xh_ * 2 + xl_, y_, c)

    def plane_row(*d):
        y_, xh_, xl_ = plane_at(*d)
        return y_ * 4 + xh_ * 2 + xl_

    def z_dev(dz):
        return dev((z + dz) % 8, x, y, c)

    barrier = pltpu.get_barrier_semaphore()
    for peer in [sib] + [plane_dev(*d) for d in plane] + [z_dev(d) for d in zline]:
        pl.semaphore_signal(barrier, inc=1, device_id=peer, device_id_type=MESH)

    loads = [
        pltpu.make_async_copy(g_hbm, g, load_s.at[0]),
        pltpu.make_async_copy(a_hbm, agat.at[col], load_s.at[1]),
        pltpu.make_async_copy(e_hbm.at[0], e, load_s.at[2]),
        pltpu.make_async_copy(a_hbm.at[:, pl.ds(pl.multiple_of(xl * 128, 128), 128)], abuf.at[xl], load_s.at[3]),
    ]
    for copy in loads:
        copy.start()

    sent = []

    def send(src, dst, s, r, to, keep=True):
        copy = pltpu.make_async_remote_copy(src_ref=src, dst_ref=dst, send_sem=s, recv_sem=r, device_id=to, device_id_type=MESH)
        copy.start()
        if keep:
            sent.append(copy)
        return copy

    loads[0].wait()
    q_hi, q_lo = split(start_factor(seed_ref[0], col * 512))
    qhl[pl.ds(0, RANK), :] = q_hi
    qhl[pl.ds(RANK, RANK), :] = q_lo
    u = fold(dot(qhl[...], g[...], NT))
    for i in range(4):
        for j in range(4):
            upart[j % 2, i * 2 + j // 2] = u[8 * i : 8 * i + 8, 256 * j : 256 * j + 256]
    loads[1].wait()
    loads[3].wait()
    pl.semaphore_wait(barrier, 1 + len(plane) + len(zline))

    yp, ym = (y + 1) % 4, (y + 3) % 4
    up, down, mirror = dev(z, x, yp, c), dev(z, x, ym, c), dev(z, (x + 2) % 4, y, c)

    def block(y_, xh_):
        return (y_ * 2 + xh_) * 2 + c

    own, b_up, b_down, b_far = col, block(yp, xh), block(ym, xh), block((y + 2) % 4, xh)
    m_own, m_up, m_down, m_far = block(y, 1 - xh), block(yp, 1 - xh), block(ym, 1 - xh), block((y + 2) % 4, 1 - xh)
    blocks = dict(own=own, up=b_up, down=b_down, far=b_far, m_own=m_own, m_up=m_up, m_down=m_down, m_far=m_far)
    slots = list(blocks)
    lanes = (up, down, mirror)
    there = (
        dict(own="down", down="far", m_own="m_down", m_down="m_far"),
        dict(own="up", up="far", m_own="m_up", m_up="m_far"),
        dict(own="m_own", far="m_far"),
    )
    moves, passed = {}, {}

    def piece(b, j):
        return agat.at[b, pl.ds(j * ROWS, ROWS)]

    def to_sib(name, j):
        at, n = piece(blocks[name], j), slots.index(name)
        passed[name, j] = send(at, at, ss.at[n, j], sr.at[n, j], sib)

    def go(lane, name, j):
        at, n = piece(blocks[name], j), sum(1 for m in moves if m[0] == lane)
        moves[lane, there[lane][name], j] = send(at, at, gs.at[lane, n], gr.at[lane, n], lanes[lane])

    def got(lane, name, j):
        moves[lane, name, j].wait_recv()
        to_sib(name, j)

    def swap(n):
        rows = pl.ds(n * ROWS, ROWS)
        return send(
            a_hbm.at[rows, pl.ds(pl.multiple_of((1 - xl) * 128, 128), 128)], abuf.at[xl, rows], swap_s.at[n], swap_s.at[CHUNKS + n],
            dev(z, xh * 2 + 1 - xl, y, c),
        )

    u_sib = send(upart.at[other], usib, us.at[0], ur.at[0], sib)
    for j in range(CHUNKS):
        to_sib("own", j)

    def product(b):
        at = pl.ds(pl.multiple_of(b * 256, 256), 256)
        comb[at, :] = dot(agat[b], g[...], TN) + e[at, :].astype(F32)

    def both(name):
        b = blocks[name]
        product(b)
        for j in range(CHUNKS):
            passed[name, j].wait_recv()
        product(b - c + other)

    u_sib.wait_recv()
    ubuf[pl.ds(0, 8)] = upart[c] + usib[...]
    k = y * 2 + xh
    ru = [send(ubuf.at[plane_row(*d) // 2], ubuf.at[8 + k], rus.at[n], rur.at[n], plane_dev(*d)) for n, d in enumerate(colp)]
    ubuf[8 + k] = ubuf[k]
    go(0, "own", 2)
    go(1, "own", 0)
    swaps = [swap(0), swap(1)]
    loads[2].wait()
    for b in range(16):
        r = fold(dot(qhl[...], e[pl.ds(b * 256, 256), :], NT))
        part[b % 2, (b // 2) * 2] = r[:, :128]
        part[b % 2, (b // 2) * 2 + 1] = r[:, 128:]
    e_sib = send(part.at[other], sibbuf, es.at[0], er.at[0], sib)
    for copy in ru:
        copy.wait_recv()
    total = ubuf[8]
    for n in range(1, 8):
        total = total + ubuf[8 + n]
    agu[c, p] = total
    au = [send(agu.at[c, p], agu.at[c, p], aus.at[n], aur.at[n], plane_dev(*d)) for n, d in enumerate(plane)]
    e_sib.wait_recv()
    part[c] = part[c] + sibbuf[...]
    re = [send(part.at[c, plane_row(*d)], rsbuf.at[p], rss.at[n], rsr.at[n], plane_dev(*d)) for n, d in enumerate(plane)]
    rsbuf[p] = part[c, p]
    swaps += [swap(2), swap(3)]
    for n, j in enumerate((3, 0, 1)):
        go(0, "own", j)
        go(1, "own", (1, 2, 3)[n])
        go(2, "own", n)
    got(0, "down", 2)
    got(1, "up", 0)
    go(0, "down", 2)
    go(1, "up", 0)
    for copy in au:
        copy.wait_recv()
    u_fwd = send(agu.at[c], agu.at[c], uss.at[0], usr.at[0], sib)
    for copy in re:
        copy.wait_recv()
    acc = rsbuf[0]
    for n in range(1, 16):
        acc = acc + rsbuf[n]
    for copy in swaps:
        copy.wait_recv()
    u_fwd.wait_recv()
    for r in range(2):
        ut = jnp.concatenate(
            [jnp.concatenate([agu[j % 2, i * 4 + (j // 2) * 2 + r] for j in range(4)], axis=1) for i in range(4)], axis=0
        )
        acc = acc + fold(dot(jnp.concatenate(split(ut), axis=0), abuf[r], NN))
    zbuf[z] = acc
    zc = [send(zbuf.at[z], zbuf.at[z], zs.at[n], zr.at[n], z_dev(d)) for n, d in enumerate(zline)]
    both("own")
    got(0, "down", 3)
    got(1, "up", 1)
    got(2, "m_own", 0)
    for copy in zc:
        copy.wait_recv()
    total = zbuf[0]
    for n in range(1, 8):
        total = total + zbuf[n]
    mine = pall.at[c, xh, y * 2 + xl]
    mine[...] = total
    pc = [send(mine, mine, ps.at[n], pr.at[n], plane_dev(*d)) for n, d in enumerate(near)]
    go(0, "down", 3)
    go(1, "up", 1)
    pf = [send(mine, mine, ps.at[7 + n], pr.at[7 + n], plane_dev(*d)) for n, d in enumerate(far)]
    go(2, "own", 3)
    for n, j in enumerate((0, 1)):
        got(0, "down", j)
        got(1, "up", j + 2)
        got(2, "m_own", j + 1)
    for j in range(3):
        go(0, "m_own", j)
        go(1, "m_own", j)
    got(0, "far", 2)
    got(1, "far", 0)
    go(2, "far", 2)

    def left_part(half):
        for cc in range(2):
            for yy in range(4):
                for ll in range(2):
                    at = pl.ds(pl.multiple_of((((yy * 2 + half) * 2 + cc) * 2 + ll) * 128, 128), 128)
                    v = pall[cc, half, yy * 2 + ll]
                    hi, lo = split(v)
                    pt[:, at] = v
                    p64[pl.ds(0, RANK), at] = hi
                    p64[pl.ds(RANK, RANK), at] = lo

    for copy in pc:
        copy.wait_recv()
    p_fwd = send(pall.at[c, xh], pall.at[c, xh], pss.at[0], psr.at[0], sib)
    both("up")
    p_fwd.wait_recv()
    left_part(xh)
    got(0, "far", 3)
    got(1, "far", 1)

    v = jnp.zeros((2 * RANK, TOK), F32)
    for name in ("own", "up", "down", "far"):
        for b in (blocks[name], blocks[name] - c + other):
            if name in ("down", "far") and b is not blocks[name]:
                for j in range(CHUNKS):
                    passed[name, j].wait_recv()
            v = v + dot(p64[:, pl.ds(pl.multiple_of(b * 256, 256), 256)], agat[b], NT)
    v = fold(v)
    for h in range(2):
        vown[h] = v[:, h * 512 : h * 512 + 512]
    v_far = send(vown.at[c], vmir.at[c], vs.at[0], vr.at[0], mirror)
    go(2, "far", 3)
    for copy in pf:
        copy.wait_recv()
    p_fwd = send(pall.at[c, 1 - xh], pall.at[c, 1 - xh], pss.at[1], psr.at[1], sib)
    for name in ("down", "far"):
        product(blocks[name])
        product(blocks[name] - c + other)
    got(2, "m_own", 3)
    go(0, "m_own", 3)
    go(1, "m_own", 3)
    p_fwd.wait_recv()
    left_part(1 - xh)
    w = fold(dot(p64[...], e[...], NN))
    got(0, "m_down", 0)
    got(1, "m_up", 0)
    v_far.wait_recv()
    v_fwd = send(vmir.at[c], vmir.at[c], vs.at[1], vr.at[1], sib)
    got(0, "m_down", 1)
    got(1, "m_up", 1)
    go(0, "m_down", 0)
    go(1, "m_up", 1)
    both("m_own")
    v_fwd.wait_recv()
    for h in range(2):
        w = w + fold(dot(jnp.concatenate(split(vown[h] + vmir[h]), axis=0), g[pl.ds(h * 512, 512), :], NN))
    for i in range(4):
        for j in range(4):
            wpart[i * 4 + j] = w[8 * i : 8 * i + 8, 128 * j : 128 * j + 128]

    def rep_dev(dx, dz):
        return dev((z + dz) % 8, xh * 2 + (xl + dx) % 2, y, c)

    wc = [
        send(wpart.at[((z + dz) % 8) * 2 + (xl + dx) % 2], wbuf.at[rep], ws.at[n], wr.at[n], rep_dev(dx, dz))
        for n, (dx, dz) in enumerate(repp)
    ]
    wbuf[rep] = wpart[rep]
    inverse = lower_inverse(dot(pt[...], pt[...], NT, precision=HIGH))
    basis = dot(inverse, pt[...], NN, precision=HIGH)
    for copy in wc:
        copy.wait_recv()
    total = wbuf[0]
    for n in range(1, 16):
        total = total + wbuf[n]
    wall[rep] = total
    wa = [send(wall.at[rep], wall.at[rep], was.at[n], war.at[n], rep_dev(dx, dz)) for n, (dx, dz) in enumerate(repp)]
    pt_out[...] = basis * 64.0
    b_hi, b_lo = split(basis)
    b96[pl.ds(0, RANK), :] = b_hi
    b96[pl.ds(RANK, RANK), :] = b_lo
    b96[pl.ds(2 * RANK, RANK), :] = b_hi
    for j in (2, 3):
        got(0, "m_down", j)
        got(1, "m_up", j)
        got(2, "m_far", j)
    both("m_up")
    both("m_down")
    got(0, "m_far", 0)
    got(1, "m_far", 1)
    both("m_far")
    for copy in wa:
        copy.wait_recv()
    w = jnp.concatenate([jnp.concatenate([wall[i * 4 + j] for j in range(4)], axis=1) for i in range(4)], axis=0)
    qt = dot(inverse, w, NN, precision=HIGH) * (1.0 / 16.0)
    qt_out[...] = qt
    f_hi, f_lo = split(qt)
    q96[pl.ds(0, RANK), :] = f_hi
    q96[pl.ds(RANK, RANK), :] = f_hi
    q96[pl.ds(2 * RANK, RANK), :] = f_lo
    for copy in sent:
        copy.wait_send()


def finish(comb, b96, q96, basis, factor, err_hbm, basis_hbm, factor_hbm, rounded, sems):
    copies = [pltpu.make_async_copy(basis, basis_hbm, sems.at[0]), pltpu.make_async_copy(factor, factor_hbm, sems.at[1])]
    for copy in copies:
        copy.start()
    step = 4096 // PIECES
    for b in range(PIECES):
        at = pl.ds(b * step, step)
        rounded[at, :] = (comb[at, :] - dot(b96[:, at], q96[...], TN)).astype(BF16)
        copies.append(pltpu.make_async_copy(rounded.at[at], err_hbm.at[0, at], sems.at[2 + b]))
        copies[-1].start()
    for copy in copies:
        copy.wait()


def local(activations, out_grads, carried_error, seed_value):
    vmem, any_ = pl.BlockSpec(memory_space=pltpu.VMEM), pl.BlockSpec(memory_space=pl.ANY)
    dma, shape = pltpu.SemaphoreType.DMA, jax.ShapeDtypeStruct
    V = pltpu.VMEM
    held = pl.pallas_call(
        kernel,
        name="round",
        out_shape=(V((4096, 512), F32), V((3 * RANK, 4096), BF16), V((3 * RANK, 512), BF16), V((RANK, 4096), F32), V((RANK, 512), F32)),
        in_specs=[pl.BlockSpec(memory_space=pltpu.SMEM), any_, any_, any_],
        out_specs=(vmem,) * 5,
        scratch_shapes=[
            V((4096, 512), BF16), V((TOK, 512), BF16), V((16, TOK, 256), BF16), V((2, TOK, 128), BF16),
            V((2 * RANK, 512), BF16), V((2, 16, RANK, 128), F32), V((16, RANK, 128), F32), V((16, RANK, 128), F32),
            V((2, 8, 8, 256), F32), V((8, 8, 256), F32), V((16, 8, 256), F32), V((2, 16, 8, 256), F32),
            V((8, RANK, 128), F32), V((2, 2, 8, RANK, 128), F32), V((RANK, 4096), F32), V((2 * RANK, 4096), BF16),
            V((16, 8, 128), F32), V((16, 8, 128), F32), V((16, 8, 128), F32),
            V((2, RANK, 512), F32), V((2, RANK, 512), F32),
            dma((4,)), dma((3, 11)), dma((3, 11)), dma((8, CHUNKS)), dma((8, CHUNKS)), dma((2 * CHUNKS,)),
            dma((1,)), dma((1,)), dma((7,)), dma((7,)), dma((15,)), dma((15,)), dma((1,)), dma((1,)), dma((1,)), dma((1,)),
            dma((15,)), dma((15,)), dma((7,)), dma((7,)), dma((15,)), dma((15,)), dma((2,)), dma((2,)),
            dma((15,)), dma((15,)), dma((15,)), dma((15,)), dma((2,)), dma((2,)),
        ],
        compiler_params=pltpu.CompilerParams(collective_id=1, has_side_effects=True, vmem_limit_bytes=28 << 20),
        cost_estimate=pl.CostEstimate(flops=4_600_000_000, bytes_accessed=10_000_000, transcendentals=0),
    )(seed_value, *[pltpu.with_memory_space_constraint(a, pltpu.HBM) for a in (activations, out_grads, carried_error)])
    err, pt, qt = pl.pallas_call(
        finish,
        name="finish",
        out_shape=(shape((1, 4096, 512), BF16), shape((RANK, 4096), F32), shape((RANK, 512), F32)),
        in_specs=[vmem] * 5,
        out_specs=(any_,) * 3,
        scratch_shapes=[V((4096, 512), BF16), dma((2 + PIECES,))],
        compiler_params=pltpu.CompilerParams(vmem_limit_bytes=12 << 20),
    )(*[pltpu.with_memory_space_constraint(a, pltpu.VMEM) for a in held])
    return pt.T, qt.T, err


def solution(mesh):
    return jax.shard_map(
        local,
        mesh=mesh,
        in_specs=(P("rep", "col"), P("rep", "col"), P("rep", None, "col"), P()),
        out_specs=(P(), P("col", None), P("rep", None, "col")),
        check_vma=False,
    )
```

```python
import functools

import jax
import jax.numpy as jnp
from jax import lax
from jax.experimental import pallas as pl
from jax.experimental.pallas import tpu as pltpu
from jax.sharding import PartitionSpec as P

RANK = 32
F32, BF16 = jnp.float32, jnp.bfloat16
MESH = pl.DeviceIdType.MESH
NN = (((1,), (0,)), ((), ()))
NT = (((1,), (1,)), ((), ()))
TN = (((0,), (0,)), ((), ()))
HIGH = lax.Precision.HIGHEST
CHUNKS = 4
TOK = 1024
ROWS = TOK // CHUNKS
PIECES = 8


def dot(a, b, dims, **kw):
    return lax.dot_general(a, b, dims, preferred_element_type=F32, **kw)


def split(x):
    hi = x.astype(BF16)
    return hi, (x - hi.astype(F32)).astype(BF16)


def fold(r):
    return r[:RANK] + r[RANK:]


def start_factor(seed, first):
    i = first + lax.broadcasted_iota(jnp.int32, (RANK, 512), 1)
    j = lax.broadcasted_iota(jnp.int32, (RANK, 512), 0)
    h = i * RANK + j
    h = h * 1103515245 + seed * 12345 + 7
    h = jnp.bitwise_xor(h, jnp.right_shift(h, 13))
    h = h * 747796405 + 1013904223
    h = jnp.bitwise_xor(h, jnp.right_shift(h, 16))
    return jnp.bitwise_and(h, 65535).astype(F32) / 32768.0 - 1.0


def lower_inverse(gram):
    lane = lax.broadcasted_iota(jnp.int32, (RANK, RANK), 1)
    row = lax.broadcasted_iota(jnp.int32, (RANK, RANK), 0)
    a = jnp.concatenate([gram, jnp.where(lane == row, 1.0, 0.0).astype(F32)], axis=1)
    rows = lax.broadcasted_iota(jnp.int32, (RANK, 2 * RANK), 0)
    for k in range(RANK):
        factor = jnp.where(rows > k, a[:, k : k + 1] / a[k : k + 1, k : k + 1], 0.0)
        a = a - factor * a[k : k + 1, :]
    pivots = jnp.sum(jnp.where(lane == row, a[:, :RANK], 0.0), axis=1, keepdims=True)
    return a[:, RANK:] / jnp.sqrt(pivots)


def kernel(
    seed_ref, a_hbm, g_hbm, e_hbm,
    comb, b96, q96, pt_out, qt_out,
    e, g, agat, abuf, qhl, part, sibbuf, rsbuf, upart, usib, ubuf, agu, zbuf, pall, pt, p64, wpart, wbuf, wall, vown, vmir,
    load_s, gs, gr, ss, sr, swap_s, us, ur, rus, rur, aus, aur, uss, usr, es, er, rss, rsr, zs, zr, ps, pr, pss, psr, ws, wr, was, war, vs, vr,
):
    rep, col = lax.axis_index("rep"), lax.axis_index("col")
    z, xl = rep // 2, rep % 2
    y, xh, c = col // 4, (col // 2) % 2, col % 2
    x = xh * 2 + xl
    p = y * 4 + x
    other = 1 - c

    def dev(z_, x_, y_, c_):
        return (z_ * 2 + x_ % 2, (y_ * 2 + x_ // 2) * 2 + c_)

    sib = (rep, col - c + other)
    near = [(0, 1, 2), (0, 0, 2), (0, 1, 1), (0, 1, 3), (0, 0, 1), (0, 0, 3), (0, 1, 0)]
    far = [(1, fl, dy) for dy in (2, 1, 3, 0) for fl in (0, 1)]
    plane = far + near
    colp = [d for d in plane if d[1] == 0]
    zline = [4, 3, 5, 2, 6, 1, 7]
    repp = [(dx, dz) for dz in (4, 3, 5, 2, 6, 1, 7, 0) for dx in (1, 0) if (dx, dz) != (0, 0)]

    def plane_at(fh, fl, dy):
        return (y + dy) % 4, (xh + fh) % 2, (xl + fl) % 2

    def plane_dev(*d):
        y_, xh_, xl_ = plane_at(*d)
        return dev(z, xh_ * 2 + xl_, y_, c)

    def plane_row(*d):
        y_, xh_, xl_ = plane_at(*d)
        return y_ * 4 + xh_ * 2 + xl_

    def z_dev(dz):
        return dev((z + dz) % 8, x, y, c)

    loads = [
        pltpu.make_async_copy(g_hbm, g, load_s.at[0]),
        pltpu.make_async_copy(a_hbm, agat.at[col], load_s.at[1]),
        pltpu.make_async_copy(e_hbm.at[0], e, load_s.at[2]),
        pltpu.make_async_copy(a_hbm.at[:, pl.ds(pl.multiple_of(xl * 128, 128), 128)], abuf.at[xl], load_s.at[3]),
    ]
    for copy in loads:
        copy.start()

    barrier = pltpu.get_barrier_semaphore()
    for peer in [z_dev(d) for d in zline] + [plane_dev(*d) for d in plane] + [sib]:
        pl.semaphore_signal(barrier, inc=1, device_id=peer, device_id_type=MESH)

    sent = []

    def send(src, dst, s, r, to, keep=True):
        copy = pltpu.make_async_remote_copy(src_ref=src, dst_ref=dst, send_sem=s, recv_sem=r, device_id=to, device_id_type=MESH)
        copy.start()
        if keep:
            sent.append(copy)
        return copy

    loads[0].wait()
    q_hi, q_lo = split(start_factor(seed_ref[0], col * 512))
    qhl[pl.ds(0, RANK), :] = q_hi
    qhl[pl.ds(RANK, RANK), :] = q_lo
    u = fold(dot(qhl[...], g[...], NT))
    for i in range(4):
        for j in range(4):
            upart[j % 2, i * 2 + j // 2] = u[8 * i : 8 * i + 8, 256 * j : 256 * j + 256]
    loads[1].wait()
    loads[3].wait()
    pl.semaphore_wait(barrier, 1 + len(plane) + len(zline))

    yp, ym = (y + 1) % 4, (y + 3) % 4
    up, down, mirror = dev(z, x, yp, c), dev(z, x, ym, c), dev(z, (x + 2) % 4, y, c)

    def block(y_, xh_):
        return (y_ * 2 + xh_) * 2 + c

    own, b_up, b_down, b_far = col, block(yp, xh), block(ym, xh), block((y + 2) % 4, xh)
    m_own, m_up, m_down, m_far = block(y, 1 - xh), block(yp, 1 - xh), block(ym, 1 - xh), block((y + 2) % 4, 1 - xh)
    blocks = dict(own=own, up=b_up, down=b_down, far=b_far, m_own=m_own, m_up=m_up, m_down=m_down, m_far=m_far)
    slots = list(blocks)
    lanes = (up, down, mirror)
    there = (
        dict(own="down", down="far", m_own="m_down", m_down="m_far"),
        dict(own="up", up="far", m_own="m_up", m_up="m_far"),
        dict(own="m_own", far="m_far"),
    )
    moves, passed = {}, {}

    def piece(b, j):
        return agat.at[b, pl.ds(j * ROWS, ROWS)]

    def to_sib(name, j):
        at, n = piece(blocks[name], j), slots.index(name)
        passed[name, j] = send(at, at, ss.at[n, j], sr.at[n, j], sib)

    def go(lane, name, j):
        at, n = piece(blocks[name], j), sum(1 for m in moves if m[0] == lane)
        moves[lane, there[lane][name], j] = send(at, at, gs.at[lane, n], gr.at[lane, n], lanes[lane])

    def got(lane, name, j):
        moves[lane, name, j].wait_recv()
        to_sib(name, j)

    def swap(n):
        rows = pl.ds(n * ROWS, ROWS)
        return send(
            a_hbm.at[rows, pl.ds(pl.multiple_of((1 - xl) * 128, 128), 128)], abuf.at[xl, rows], swap_s.at[n], swap_s.at[CHUNKS + n],
            dev(z, xh * 2 + 1 - xl, y, c),
        )

    u_sib = send(upart.at[other], usib, us.at[0], ur.at[0], sib)
    for j in range(CHUNKS):
        to_sib("own", j)

    def product(b):
        at = pl.ds(pl.multiple_of(b * 256, 256), 256)
        comb[at, :] = dot(agat[b], g[...], TN) + e[at, :].astype(F32)

    def both(name):
        b = blocks[name]
        product(b)
        for j in range(CHUNKS):
            passed[name, j].wait_recv()
        product(b - c + other)

    u_sib.wait_recv()
    ubuf[pl.ds(0, 8)] = upart[c] + usib[...]
    k = y * 2 + xh
    ru = [send(ubuf.at[plane_row(*d) // 2], ubuf.at[8 + k], rus.at[n], rur.at[n], plane_dev(*d)) for n, d in enumerate(colp)]
    ubuf[8 + k] = ubuf[k]
    go(0, "own", 2)
    go(1, "own", 0)
    swaps = [swap(0), swap(1)]
    loads[2].wait()
    for b in range(16):
        r = fold(dot(qhl[...], e[pl.ds(b * 256, 256), :], NT))
        part[b % 2, (b // 2) * 2] = r[:, :128]
        part[b % 2, (b // 2) * 2 + 1] = r[:, 128:]
    e_sib = send(part.at[other], sibbuf, es.at[0], er.at[0], sib)
    e_sib.wait_recv()
    part[c] = part[c] + sibbuf[...]
    re = [send(part.at[c, plane_row(*d)], rsbuf.at[p], rss.at[n], rsr.at[n], plane_dev(*d)) for n, d in enumerate(plane)]
    rsbuf[p] = part[c, p]
    for copy in ru:
        copy.wait_recv()
    total = ubuf[8]
    for n in range(1, 8):
        total = total + ubuf[8 + n]
    agu[c, p] = total
    au = [send(agu.at[c, p], agu.at[c, p], aus.at[n], aur.at[n], plane_dev(*d)) for n, d in enumerate(plane)]
    swaps += [swap(2), swap(3)]
    for n, j in enumerate((3, 0, 1)):
        go(0, "own", j)
        go(1, "own", (1, 2, 3)[n])
        go(2, "own", n)
    got(0, "down", 2)
    got(1, "up", 0)
    go(0, "down", 2)
    go(1, "up", 0)
    for copy in au:
        copy.wait_recv()
    u_fwd = send(agu.at[c], agu.at[c], uss.at[0], usr.at[0], sib)
    for copy in re:
        copy.wait_recv()
    acc = rsbuf[0]
    for n in range(1, 16):
        acc = acc + rsbuf[n]
    for copy in swaps:
        copy.wait_recv()
    u_fwd.wait_recv()
    for r in range(2):
        ut = jnp.concatenate(
            [jnp.concatenate([agu[j % 2, i * 4 + (j // 2) * 2 + r] for j in range(4)], axis=1) for i in range(4)], axis=0
        )
        acc = acc + fold(dot(jnp.concatenate(split(ut), axis=0), abuf[r], NN))
    zbuf[z] = acc
    zc = [send(zbuf.at[z], zbuf.at[z], zs.at[n], zr.at[n], z_dev(d)) for n, d in enumerate(zline)]
    both("own")
    got(0, "down", 3)
    got(1, "up", 1)
    got(2, "m_own", 0)
    for copy in zc:
        copy.wait_recv()
    total = zbuf[0]
    for n in range(1, 8):
        total = total + zbuf[n]
    mine = pall.at[c, xh, y * 2 + xl]
    mine[...] = total
    pc = [send(mine, mine, ps.at[n], pr.at[n], plane_dev(*d)) for n, d in enumerate(near)]
    go(0, "down", 3)
    go(1, "up", 1)
    pf = [send(mine, mine, ps.at[7 + n], pr.at[7 + n], plane_dev(*d)) for n, d in enumerate(far)]
    go(2, "own", 3)
    for n, j in enumerate((0, 1)):
        got(0, "down", j)
        got(1, "up", j + 2)
        got(2, "m_own", j + 1)
    for j in range(3):
        go(0, "m_own", j)
        go(1, "m_own", j)
    got(0, "far", 2)
    got(1, "far", 0)
    go(2, "far", 2)

    def left_part(half):
        for cc in range(2):
            for yy in range(4):
                for ll in range(2):
                    at = pl.ds(pl.multiple_of((((yy * 2 + half) * 2 + cc) * 2 + ll) * 128, 128), 128)
                    v = pall[cc, half, yy * 2 + ll]
                    hi, lo = split(v)
                    pt[:, at] = v
                    p64[pl.ds(0, RANK), at] = hi
                    p64[pl.ds(RANK, RANK), at] = lo

    for copy in pc:
        copy.wait_recv()
    p_fwd = send(pall.at[c, xh], pall.at[c, xh], pss.at[0], psr.at[0], sib)
    both("up")
    p_fwd.wait_recv()
    left_part(xh)
    got(0, "far", 3)
    got(1, "far", 1)

    v = jnp.zeros((2 * RANK, TOK), F32)
    for name in ("own", "up", "down", "far"):
        for b in (blocks[name], blocks[name] - c + other):
            if name in ("down", "far") and b is not blocks[name]:
                for j in range(CHUNKS):
                    passed[name, j].wait_recv()
            v = v + dot(p64[:, pl.ds(pl.multiple_of(b * 256, 256), 256)], agat[b], NT)
    v = fold(v)
    for h in range(2):
        vown[h] = v[:, h * 512 : h * 512 + 512]
    v_far = send(vown.at[c], vmir.at[c], vs.at[0], vr.at[0], mirror)
    go(2, "far", 3)
    for copy in pf:
        copy.wait_recv()
    p_fwd = send(pall.at[c, 1 - xh], pall.at[c, 1 - xh], pss.at[1], psr.at[1], sib)
    for name in ("down", "far"):
        product(blocks[name])
        product(blocks[name] - c + other)
    got(2, "m_own", 3)
    p_fwd.wait_recv()
    left_part(1 - xh)
    w = fold(dot(p64[...], e[...], NN))
    got(0, "m_down", 0)
    got(1, "m_up", 0)
    v_far.wait_recv()
    v_fwd = send(vmir.at[c], vmir.at[c], vs.at[1], vr.at[1], sib)
    got(0, "m_down", 1)
    got(1, "m_up", 1)
    go(0, "m_down", 0)
    go(1, "m_up", 1)
    go(0, "m_own", 3)
    go(1, "m_own", 3)
    both("m_own")
    v_fwd.wait_recv()
    for h in range(2):
        w = w + fold(dot(jnp.concatenate(split(vown[h] + vmir[h]), axis=0), g[pl.ds(h * 512, 512), :], NN))
    for i in range(4):
        for j in range(4):
            wpart[i * 4 + j] = w[8 * i : 8 * i + 8, 128 * j : 128 * j + 128]

    def rep_dev(dx, dz):
        return dev((z + dz) % 8, xh * 2 + (xl + dx) % 2, y, c)

    wc = [
        send(wpart.at[((z + dz) % 8) * 2 + (xl + dx) % 2], wbuf.at[rep], ws.at[n], wr.at[n], rep_dev(dx, dz))
        for n, (dx, dz) in enumerate(repp)
    ]
    wbuf[rep] = wpart[rep]
    inverse = lower_inverse(dot(pt[...], pt[...], NT, precision=HIGH))
    basis = dot(inverse, pt[...], NN, precision=HIGH)
    pt_out[...] = basis * 64.0
    b_hi, b_lo = split(basis)
    b96[pl.ds(0, RANK), :] = b_hi
    b96[pl.ds(RANK, RANK), :] = b_lo
    b96[pl.ds(2 * RANK, RANK), :] = b_hi
    got(2, "m_far", 2)
    got(0, "m_down", 2)
    got(1, "m_up", 2)
    for copy in wc:
        copy.wait_recv()
    total = wbuf[0]
    for n in range(1, 16):
        total = total + wbuf[n]
    wall[rep] = total
    wa = [send(wall.at[rep], wall.at[rep], was.at[n], war.at[n], rep_dev(dx, dz)) for n, (dx, dz) in enumerate(repp)]
    got(0, "m_down", 3)
    got(1, "m_up", 3)
    got(2, "m_far", 3)
    got(0, "m_far", 0)
    got(1, "m_far", 1)
    both("m_up")
    both("m_down")
    both("m_far")
    for copy in wa:
        copy.wait_recv()
    w = jnp.concatenate([jnp.concatenate([wall[i * 4 + j] for j in range(4)], axis=1) for i in range(4)], axis=0)
    qt = dot(inverse, w, NN, precision=HIGH) * (1.0 / 16.0)
    qt_out[...] = qt
    f_hi, f_lo = split(qt)
    q96[pl.ds(0, RANK), :] = f_hi
    q96[pl.ds(RANK, RANK), :] = f_hi
    q96[pl.ds(2 * RANK, RANK), :] = f_lo
    for copy in sent:
        copy.wait_send()


def finish(comb, b96, q96, basis, factor, err_hbm, basis_hbm, factor_hbm, rounded, sems):
    copies = [pltpu.make_async_copy(basis, basis_hbm, sems.at[0]), pltpu.make_async_copy(factor, factor_hbm, sems.at[1])]
    for copy in copies:
        copy.start()
    step = 4096 // PIECES
    for b in range(PIECES):
        at = pl.ds(b * step, step)
        rounded[at, :] = (comb[at, :] - dot(b96[:, at], q96[...], TN)).astype(BF16)
        copies.append(pltpu.make_async_copy(rounded.at[at], err_hbm.at[0, at], sems.at[2 + b]))
        copies[-1].start()
    for copy in copies:
        copy.wait()


def local(activations, out_grads, carried_error, seed_value):
    vmem, any_ = pl.BlockSpec(memory_space=pltpu.VMEM), pl.BlockSpec(memory_space=pl.ANY)
    dma, shape = pltpu.SemaphoreType.DMA, jax.ShapeDtypeStruct
    V = pltpu.VMEM
    held = pl.pallas_call(
        kernel,
        name="round",
        out_shape=(V((4096, 512), F32), V((3 * RANK, 4096), BF16), V((3 * RANK, 512), BF16), V((RANK, 4096), F32), V((RANK, 512), F32)),
        in_specs=[pl.BlockSpec(memory_space=pltpu.SMEM), any_, any_, any_],
        out_specs=(vmem,) * 5,
        scratch_shapes=[
            V((4096, 512), BF16), V((TOK, 512), BF16), V((16, TOK, 256), BF16), V((2, TOK, 128), BF16),
            V((2 * RANK, 512), BF16), V((2, 16, RANK, 128), F32), V((16, RANK, 128), F32), V((16, RANK, 128), F32),
            V((2, 8, 8, 256), F32), V((8, 8, 256), F32), V((16, 8, 256), F32), V((2, 16, 8, 256), F32),
            V((8, RANK, 128), F32), V((2, 2, 8, RANK, 128), F32), V((RANK, 4096), F32), V((2 * RANK, 4096), BF16),
            V((16, 8, 128), F32), V((16, 8, 128), F32), V((16, 8, 128), F32),
            V((2, RANK, 512), F32), V((2, RANK, 512), F32),
            dma((4,)), dma((3, 11)), dma((3, 11)), dma((8, CHUNKS)), dma((8, CHUNKS)), dma((2 * CHUNKS,)),
            dma((1,)), dma((1,)), dma((7,)), dma((7,)), dma((15,)), dma((15,)), dma((1,)), dma((1,)), dma((1,)), dma((1,)),
            dma((15,)), dma((15,)), dma((7,)), dma((7,)), dma((15,)), dma((15,)), dma((2,)), dma((2,)),
            dma((15,)), dma((15,)), dma((15,)), dma((15,)), dma((2,)), dma((2,)),
        ],
        compiler_params=pltpu.CompilerParams(collective_id=1, has_side_effects=True, vmem_limit_bytes=28 << 20),
        cost_estimate=pl.CostEstimate(flops=4_600_000_000, bytes_accessed=10_000_000, transcendentals=0),
    )(seed_value, *[pltpu.with_memory_space_constraint(a, pltpu.HBM) for a in (activations, out_grads, carried_error)])
    err, pt, qt = pl.pallas_call(
        finish,
        name="finish",
        out_shape=(shape((1, 4096, 512), BF16), shape((RANK, 4096), F32), shape((RANK, 512), F32)),
        in_specs=[vmem] * 5,
        out_specs=(any_,) * 3,
        scratch_shapes=[V((4096, 512), BF16), dma((2 + PIECES,))],
        compiler_params=pltpu.CompilerParams(vmem_limit_bytes=12 << 20),
    )(*[pltpu.with_memory_space_constraint(a, pltpu.VMEM) for a in held])
    return pt.T, qt.T, err


def solution(mesh):
    return jax.shard_map(
        local,
        mesh=mesh,
        in_specs=(P("rep", "col"), P("rep", "col"), P("rep", None, "col"), P()),
        out_specs=(P(), P("col", None), P("rep", None, "col")),
        check_vma=False,
    )
```

```python
import functools

import jax
import jax.numpy as jnp
from jax import lax
from jax.experimental import pallas as pl
from jax.experimental.pallas import tpu as pltpu
from jax.sharding import PartitionSpec as P

RANK = 32
F32, BF16 = jnp.float32, jnp.bfloat16
MESH = pl.DeviceIdType.MESH
NN = (((1,), (0,)), ((), ()))
NT = (((1,), (1,)), ((), ()))
TN = (((0,), (0,)), ((), ()))
HIGH = lax.Precision.HIGHEST
CHUNKS = 4
TOK = 1024
ROWS = TOK // CHUNKS
PIECES = 8


def dot(a, b, dims, **kw):
    return lax.dot_general(a, b, dims, preferred_element_type=F32, **kw)


def split(x):
    hi = x.astype(BF16)
    return hi, (x - hi.astype(F32)).astype(BF16)


def fold(r):
    return r[:RANK] + r[RANK:]


def start_factor(seed, first):
    i = first + lax.broadcasted_iota(jnp.int32, (RANK, 512), 1)
    j = lax.broadcasted_iota(jnp.int32, (RANK, 512), 0)
    h = i * RANK + j
    h = h * 1103515245 + seed * 12345 + 7
    h = jnp.bitwise_xor(h, jnp.right_shift(h, 13))
    h = h * 747796405 + 1013904223
    h = jnp.bitwise_xor(h, jnp.right_shift(h, 16))
    return jnp.bitwise_and(h, 65535).astype(F32) / 32768.0 - 1.0


def lower_inverse(gram):
    lane = lax.broadcasted_iota(jnp.int32, (RANK, RANK), 1)
    row = lax.broadcasted_iota(jnp.int32, (RANK, RANK), 0)
    a = jnp.concatenate([gram, jnp.where(lane == row, 1.0, 0.0).astype(F32)], axis=1)
    rows = lax.broadcasted_iota(jnp.int32, (RANK, 2 * RANK), 0)
    for k in range(RANK):
        factor = jnp.where(rows > k, a[:, k : k + 1] / a[k : k + 1, k : k + 1], 0.0)
        a = a - factor * a[k : k + 1, :]
    pivots = jnp.sum(jnp.where(lane == row, a[:, :RANK], 0.0), axis=1, keepdims=True)
    return a[:, RANK:] / jnp.sqrt(pivots)


def kernel(
    seed_ref, a_hbm, g_hbm, e_hbm,
    comb, b96, q96, pt_out, qt_out,
    e, g, agat, abuf, qhl, part, sibbuf, rsbuf, upart, usib, ubuf, agu, zbuf, pall, pt, p64, wpart, wbuf, wall, vown, vmir,
    load_s, gs, gr, ss, sr, swap_s, us, ur, rus, rur, aus, aur, uss, usr, es, er, rss, rsr, zs, zr, ps, pr, pss, psr, ws, wr, was, war, vs, vr,
):
    rep, col = lax.axis_index("rep"), lax.axis_index("col")
    z, xl = rep // 2, rep % 2
    y, xh, c = col // 4, (col // 2) % 2, col % 2
    x = xh * 2 + xl
    p = y * 4 + x
    other = 1 - c

    def dev(z_, x_, y_, c_):
        return (z_ * 2 + x_ % 2, (y_ * 2 + x_ // 2) * 2 + c_)

    sib = (rep, col - c + other)
    near = [(0, 1, 2), (0, 0, 2), (0, 1, 1), (0, 1, 3), (0, 0, 1), (0, 0, 3), (0, 1, 0)]
    far = [(1, fl, dy) for dy in (2, 1, 3, 0) for fl in (0, 1)]
    plane = far + near
    colp = [d for d in plane if d[1] == 0]
    zline = [4, 3, 5, 2, 6, 1, 7]
    repp = [(dx, dz) for dz in (4, 3, 5, 2, 6, 1, 7, 0) for dx in (1, 0) if (dx, dz) != (0, 0)]

    def plane_at(fh, fl, dy):
        return (y + dy) % 4, (xh + fh) % 2, (xl + fl) % 2

    def plane_dev(*d):
        y_, xh_, xl_ = plane_at(*d)
        return dev(z, xh_ * 2 + xl_, y_, c)

    def plane_row(*d):
        y_, xh_, xl_ = plane_at(*d)
        return y_ * 4 + xh_ * 2 + xl_

    def z_dev(dz):
        return dev((z + dz) % 8, x, y, c)

    loads = [
        pltpu.make_async_copy(g_hbm, g, load_s.at[0]),
        pltpu.make_async_copy(a_hbm, agat.at[col], load_s.at[1]),
        pltpu.make_async_copy(e_hbm.at[0], e, load_s.at[2]),
        pltpu.make_async_copy(a_hbm.at[:, pl.ds(pl.multiple_of(xl * 128, 128), 128)], abuf.at[xl], load_s.at[3]),
    ]
    for copy in loads:
        copy.start()

    barrier = pltpu.get_barrier_semaphore()
    for peer in [z_dev(d) for d in zline] + [plane_dev(*d) for d in plane] + [sib]:
        pl.semaphore_signal(barrier, inc=1, device_id=peer, device_id_type=MESH)

    sent = []

    def send(src, dst, s, r, to, keep=True):
        copy = pltpu.make_async_remote_copy(src_ref=src, dst_ref=dst, send_sem=s, recv_sem=r, device_id=to, device_id_type=MESH)
        copy.start()
        if keep:
            sent.append(copy)
        return copy

    loads[0].wait()
    q_hi, q_lo = split(start_factor(seed_ref[0], col * 512))
    qhl[pl.ds(0, RANK), :] = q_hi
    qhl[pl.ds(RANK, RANK), :] = q_lo
    u = fold(dot(qhl[...], g[...], NT))
    for i in range(4):
        for j in range(4):
            upart[j % 2, i * 2 + j // 2] = u[8 * i : 8 * i + 8, 256 * j : 256 * j + 256]
    loads[1].wait()
    loads[3].wait()
    pl.semaphore_wait(barrier, 1 + len(plane) + len(zline))

    yp, ym = (y + 1) % 4, (y + 3) % 4
    up, down, mirror = dev(z, x, yp, c), dev(z, x, ym, c), dev(z, (x + 2) % 4, y, c)

    def block(y_, xh_):
        return (y_ * 2 + xh_) * 2 + c

    own, b_up, b_down, b_far = col, block(yp, xh), block(ym, xh), block((y + 2) % 4, xh)
    m_own, m_up, m_down, m_far = block(y, 1 - xh), block(yp, 1 - xh), block(ym, 1 - xh), block((y + 2) % 4, 1 - xh)
    blocks = dict(own=own, up=b_up, down=b_down, far=b_far, m_own=m_own, m_up=m_up, m_down=m_down, m_far=m_far)
    slots = list(blocks)
    lanes = (up, down, mirror)
    there = (
        dict(own="down", down="far", m_own="m_down", m_down="m_far"),
        dict(own="up", up="far", m_own="m_up", m_up="m_far"),
        dict(own="m_own", far="m_far"),
    )
    moves, passed = {}, {}

    def piece(b, j):
        return agat.at[b, pl.ds(j * ROWS, ROWS)]

    def to_sib(name, j):
        at, n = piece(blocks[name], j), slots.index(name)
        passed[name, j] = send(at, at, ss.at[n, j], sr.at[n, j], sib)

    def go(lane, name, j):
        at, n = piece(blocks[name], j), sum(1 for m in moves if m[0] == lane)
        moves[lane, there[lane][name], j] = send(at, at, gs.at[lane, n], gr.at[lane, n], lanes[lane])

    def got(lane, name, j):
        moves[lane, name, j].wait_recv()
        to_sib(name, j)

    def swap(n):
        rows = pl.ds(n * ROWS, ROWS)
        return send(
            a_hbm.at[rows, pl.ds(pl.multiple_of((1 - xl) * 128, 128), 128)], abuf.at[xl, rows], swap_s.at[n], swap_s.at[CHUNKS + n],
            dev(z, xh * 2 + 1 - xl, y, c),
        )

    u_sib = send(upart.at[other], usib, us.at[0], ur.at[0], sib)
    for j in range(CHUNKS):
        to_sib("own", j)

    def product(b):
        at = pl.ds(pl.multiple_of(b * 256, 256), 256)
        comb[at, :] = dot(agat[b], g[...], TN) + e[at, :].astype(F32)

    def both(name):
        b = blocks[name]
        product(b)
        for j in range(CHUNKS):
            passed[name, j].wait_recv()
        product(b - c + other)

    u_sib.wait_recv()
    ubuf[pl.ds(0, 8)] = upart[c] + usib[...]
    k = y * 2 + xh
    ru = [send(ubuf.at[plane_row(*d) // 2], ubuf.at[8 + k], rus.at[n], rur.at[n], plane_dev(*d)) for n, d in enumerate(colp)]
    ubuf[8 + k] = ubuf[k]
    go(0, "own", 2)
    go(1, "own", 0)
    swaps = [swap(0), swap(1)]
    loads[2].wait()
    for b in range(16):
        r = fold(dot(qhl[...], e[pl.ds(b * 256, 256), :], NT))
        part[b % 2, (b // 2) * 2] = r[:, :128]
        part[b % 2, (b // 2) * 2 + 1] = r[:, 128:]
    e_sib = send(part.at[other], sibbuf, es.at[0], er.at[0], sib)
    e_sib.wait_recv()
    part[c] = part[c] + sibbuf[...]
    re = [send(part.at[c, plane_row(*d)], rsbuf.at[p], rss.at[n], rsr.at[n], plane_dev(*d)) for n, d in enumerate(plane)]
    rsbuf[p] = part[c, p]
    for copy in ru:
        copy.wait_recv()
    total = ubuf[8]
    for n in range(1, 8):
        total = total + ubuf[8 + n]
    agu[c, p] = total
    au = [send(agu.at[c, p], agu.at[c, p], aus.at[n], aur.at[n], plane_dev(*d)) for n, d in enumerate(plane)]
    swaps += [swap(2), swap(3)]
    for n, j in enumerate((3, 0, 1)):
        go(0, "own", j)
        go(1, "own", (1, 2, 3)[n])
        go(2, "own", n)
    got(0, "down", 2)
    got(1, "up", 0)
    go(0, "down", 2)
    go(1, "up", 0)
    for copy in au:
        copy.wait_recv()
    u_fwd = send(agu.at[c], agu.at[c], uss.at[0], usr.at[0], sib)
    for copy in re:
        copy.wait_recv()
    acc = rsbuf[0]
    for n in range(1, 16):
        acc = acc + rsbuf[n]
    for copy in swaps:
        copy.wait_recv()
    u_fwd.wait_recv()
    for r in range(2):
        ut = jnp.concatenate(
            [jnp.concatenate([agu[j % 2, i * 4 + (j // 2) * 2 + r] for j in range(4)], axis=1) for i in range(4)], axis=0
        )
        acc = acc + fold(dot(jnp.concatenate(split(ut), axis=0), abuf[r], NN))
    zbuf[z] = acc
    zc = [send(zbuf.at[z], zbuf.at[z], zs.at[n], zr.at[n], z_dev(d)) for n, d in enumerate(zline)]
    both("own")
    got(0, "down", 3)
    got(1, "up", 1)
    got(2, "m_own", 0)
    for copy in zc:
        copy.wait_recv()
    total = zbuf[0]
    for n in range(1, 8):
        total = total + zbuf[n]
    mine = pall.at[c, xh, y * 2 + xl]
    mine[...] = total
    pc = [send(mine, mine, ps.at[n], pr.at[n], plane_dev(*d)) for n, d in enumerate(near)]
    go(0, "down", 3)
    go(1, "up", 1)
    pf = [send(mine, mine, ps.at[7 + n], pr.at[7 + n], plane_dev(*d)) for n, d in enumerate(far)]
    go(2, "own", 3)
    for n, j in enumerate((0, 1)):
        got(0, "down", j)
        got(1, "up", j + 2)
        got(2, "m_own", j + 1)
    for j in range(3):
        go(0, "m_own", j)
        go(1, "m_own", j)
    got(0, "far", 2)
    got(1, "far", 0)
    go(2, "far", 2)

    def left_part(half):
        for cc in range(2):
            for yy in range(4):
                for ll in range(2):
                    at = pl.ds(pl.multiple_of((((yy * 2 + half) * 2 + cc) * 2 + ll) * 128, 128), 128)
                    v = pall[cc, half, yy * 2 + ll]
                    hi, lo = split(v)
                    pt[:, at] = v
                    p64[pl.ds(0, RANK), at] = hi
                    p64[pl.ds(RANK, RANK), at] = lo

    for copy in pc:
        copy.wait_recv()
    p_fwd = send(pall.at[c, xh], pall.at[c, xh], pss.at[0], psr.at[0], sib)
    both("up")
    p_fwd.wait_recv()
    left_part(xh)
    got(0, "far", 3)
    got(1, "far", 1)

    v = jnp.zeros((2 * RANK, TOK), F32)
    for name in ("own", "up", "down", "far"):
        for b in (blocks[name], blocks[name] - c + other):
            if name in ("down", "far") and b is not blocks[name]:
                for j in range(CHUNKS):
                    passed[name, j].wait_recv()
            v = v + dot(p64[:, pl.ds(pl.multiple_of(b * 256, 256), 256)], agat[b], NT)
    v = fold(v)
    for h in range(2):
        vown[h] = v[:, h * 512 : h * 512 + 512]
    v_far = send(vown.at[c], vmir.at[c], vs.at[0], vr.at[0], mirror)
    go(2, "far", 3)
    for copy in pf:
        copy.wait_recv()
    p_fwd = send(pall.at[c, 1 - xh], pall.at[c, 1 - xh], pss.at[1], psr.at[1], sib)
    for name in ("down", "far"):
        product(blocks[name])
        product(blocks[name] - c + other)
    got(2, "m_own", 3)
    p_fwd.wait_recv()
    left_part(1 - xh)
    w = fold(dot(p64[...], e[...], NN))
    got(0, "m_down", 0)
    got(1, "m_up", 0)
    v_far.wait_recv()
    def times_grads(h):
        tokens = pl.ds(pl.multiple_of(h * 512, 512), 512)
        return fold(dot(jnp.concatenate(split(vown[h] + vmir[h]), axis=0), g[tokens, :], NN))

    v_fwd = send(vmir.at[c], vmir.at[c], vs.at[1], vr.at[1], sib)
    got(0, "m_down", 1)
    got(1, "m_up", 1)
    go(0, "m_down", 0)
    go(1, "m_up", 1)
    go(0, "m_own", 3)
    go(1, "m_own", 3)
    both("m_own")
    w = w + times_grads(c)
    v_fwd.wait_recv()
    w = w + times_grads(other)
    for i in range(4):
        for j in range(4):
            wpart[i * 4 + j] = w[8 * i : 8 * i + 8, 128 * j : 128 * j + 128]

    def rep_dev(dx, dz):
        return dev((z + dz) % 8, xh * 2 + (xl + dx) % 2, y, c)

    wc = [
        send(wpart.at[((z + dz) % 8) * 2 + (xl + dx) % 2], wbuf.at[rep], ws.at[n], wr.at[n], rep_dev(dx, dz))
        for n, (dx, dz) in enumerate(repp)
    ]
    wbuf[rep] = wpart[rep]
    inverse = lower_inverse(dot(pt[...], pt[...], NT, precision=HIGH))
    basis = dot(inverse, pt[...], NN, precision=HIGH)
    pt_out[...] = basis * 64.0
    b_hi, b_lo = split(basis)
    b96[pl.ds(0, RANK), :] = b_hi
    b96[pl.ds(RANK, RANK), :] = b_lo
    b96[pl.ds(2 * RANK, RANK), :] = b_hi
    got(2, "m_far", 2)
    got(0, "m_down", 2)
    got(1, "m_up", 2)
    for copy in wc:
        copy.wait_recv()
    total = wbuf[0]
    for n in range(1, 16):
        total = total + wbuf[n]
    wall[rep] = total
    wa = [send(wall.at[rep], wall.at[rep], was.at[n], war.at[n], rep_dev(dx, dz)) for n, (dx, dz) in enumerate(repp)]
    got(0, "m_down", 3)
    got(1, "m_up", 3)
    got(2, "m_far", 3)
    got(0, "m_far", 0)
    got(1, "m_far", 1)
    both("m_up")
    both("m_down")
    both("m_far")
    for copy in wa:
        copy.wait_recv()
    w = jnp.concatenate([jnp.concatenate([wall[i * 4 + j] for j in range(4)], axis=1) for i in range(4)], axis=0)
    qt = dot(inverse, w, NN, precision=HIGH) * (1.0 / 16.0)
    qt_out[...] = qt
    f_hi, f_lo = split(qt)
    q96[pl.ds(0, RANK), :] = f_hi
    q96[pl.ds(RANK, RANK), :] = f_hi
    q96[pl.ds(2 * RANK, RANK), :] = f_lo
    for copy in sent:
        copy.wait_send()


def finish(comb, b96, q96, basis, factor, err_hbm, basis_hbm, factor_hbm, rounded, sems):
    copies = [pltpu.make_async_copy(basis, basis_hbm, sems.at[0]), pltpu.make_async_copy(factor, factor_hbm, sems.at[1])]
    for copy in copies:
        copy.start()
    step = 4096 // PIECES
    for b in range(PIECES):
        at = pl.ds(b * step, step)
        rounded[at, :] = (comb[at, :] - dot(b96[:, at], q96[...], TN)).astype(BF16)
        copies.append(pltpu.make_async_copy(rounded.at[at], err_hbm.at[0, at], sems.at[2 + b]))
        copies[-1].start()
    for copy in copies:
        copy.wait()


def local(activations, out_grads, carried_error, seed_value):
    vmem, any_ = pl.BlockSpec(memory_space=pltpu.VMEM), pl.BlockSpec(memory_space=pl.ANY)
    dma, shape = pltpu.SemaphoreType.DMA, jax.ShapeDtypeStruct
    V = pltpu.VMEM
    held = pl.pallas_call(
        kernel,
        name="round",
        out_shape=(V((4096, 512), F32), V((3 * RANK, 4096), BF16), V((3 * RANK, 512), BF16), V((RANK, 4096), F32), V((RANK, 512), F32)),
        in_specs=[pl.BlockSpec(memory_space=pltpu.SMEM), any_, any_, any_],
        out_specs=(vmem,) * 5,
        scratch_shapes=[
            V((4096, 512), BF16), V((TOK, 512), BF16), V((16, TOK, 256), BF16), V((2, TOK, 128), BF16),
            V((2 * RANK, 512), BF16), V((2, 16, RANK, 128), F32), V((16, RANK, 128), F32), V((16, RANK, 128), F32),
            V((2, 8, 8, 256), F32), V((8, 8, 256), F32), V((16, 8, 256), F32), V((2, 16, 8, 256), F32),
            V((8, RANK, 128), F32), V((2, 2, 8, RANK, 128), F32), V((RANK, 4096), F32), V((2 * RANK, 4096), BF16),
            V((16, 8, 128), F32), V((16, 8, 128), F32), V((16, 8, 128), F32),
            V((2, RANK, 512), F32), V((2, RANK, 512), F32),
            dma((4,)), dma((3, 11)), dma((3, 11)), dma((8, CHUNKS)), dma((8, CHUNKS)), dma((2 * CHUNKS,)),
            dma((1,)), dma((1,)), dma((7,)), dma((7,)), dma((15,)), dma((15,)), dma((1,)), dma((1,)), dma((1,)), dma((1,)),
            dma((15,)), dma((15,)), dma((7,)), dma((7,)), dma((15,)), dma((15,)), dma((2,)), dma((2,)),
            dma((15,)), dma((15,)), dma((15,)), dma((15,)), dma((2,)), dma((2,)),
        ],
        compiler_params=pltpu.CompilerParams(collective_id=1, has_side_effects=True, vmem_limit_bytes=28 << 20),
        cost_estimate=pl.CostEstimate(flops=4_600_000_000, bytes_accessed=10_000_000, transcendentals=0),
    )(seed_value, *[pltpu.with_memory_space_constraint(a, pltpu.HBM) for a in (activations, out_grads, carried_error)])
    err, pt, qt = pl.pallas_call(
        finish,
        name="finish",
        out_shape=(shape((1, 4096, 512), BF16), shape((RANK, 4096), F32), shape((RANK, 512), F32)),
        in_specs=[vmem] * 5,
        out_specs=(any_,) * 3,
        scratch_shapes=[V((4096, 512), BF16), dma((2 + PIECES,))],
        compiler_params=pltpu.CompilerParams(vmem_limit_bytes=12 << 20),
    )(*[pltpu.with_memory_space_constraint(a, pltpu.VMEM) for a in held])
    return pt.T, qt.T, err


def solution(mesh):
    return jax.shard_map(
        local,
        mesh=mesh,
        in_specs=(P("rep", "col"), P("rep", "col"), P("rep", None, "col"), P()),
        out_specs=(P(), P("col", None), P("rep", None, "col")),
        check_vma=False,
    )
```
